768 devices in a mesh: grp: 24 (over z, core), shard: 32 (over x, y).
Axes of the slice: x: 4, y: 8, z: 12, core: 2. Of those that a mesh axis runs over, the one named last changes fastest.
Arguments:
- points: bfloat16 [196608, 4096], P(('grp', 'shard'))
- centroids: bfloat16 [128, 168, 4096], P('shard', 'grp')
- candidates: int32 [768, 2], P('grp'), may hold values from 0 to 167
- assign: int32 [196608], P(('grp', 'shard')), may hold values from 0 to 3071, as said below
- slot_index: int32 [196608], P(('grp', 'shard')), may hold values from 0 to 127, as said below
Outputs:
- cand_scores: float32 [196608, 256], P(('grp', 'shard'))
- gram: float32 [3072, 128, 128], P(('grp', 'shard'))
- member_best: float32 [196608], P(('grp', 'shard'))
The draws below stay inside these ranges and needn't reach their ends.
Inputs may be any that keep to these rules, and one draw needn't show every extreme that they name: `candidates`: tile numbers of the candidate lists; a list may name a tile twice. `assign`: the points of group index g of grp are assigned to clusters g * 32 * 4 to (g + 1) * 32 * 4 - 1; cluster c is owned by device c // 4 in grp+shard order. The points of one device fall on the clusters of one owner at most 12 times, and on one cluster at most 12 // 4 times; both bounds are reached in every draw. `slot_index`: within one cluster the members' slot indices are distinct; every cluster uses slot 127.
All inputs are finite; a program needn't handle non-finite values.
Results may differ from the reference program's by a relative error of at most 0.0003.
Values may be sent and summed in bfloat16 or wider, within the bound.
A program may use at most 64 MiB of HBM per device.

```python
import math
import jax
import jax.numpy as jnp
import numpy as np
from jax import lax

D = 4096
TILE = 128
K = 2
CAP = 128
PTS_DEV = 256
CL_DEV = 4
SLOT = 12
NTILES = 168
NLISTS = 768
NPTS = 196608
CLUSTERS = 3072
N_GRP = 24
N_SHARD = 32


def apply_scales(key, base_field):
    row_key, column_key = jax.random.split(key)
    row_shape = base_field.shape[:-1] + (1,)
    row_scale = jnp.exp(jax.random.uniform(row_key, row_shape, jnp.float32) * math.log(10.0))
    column_scale = jnp.exp(jax.random.uniform(column_key, (base_field.shape[-1],), jnp.float32, -0.5, 0.5) * math.log(10.0))
    return base_field * row_scale * column_scale


def draw_points(key, part):
    key = jax.random.fold_in(key, 11)
    base_key, scale_key = jax.random.split(key)
    full_shape = (NPTS, D)
    base_field = jnp.clip(jax.random.normal(base_key, full_shape, jnp.float32), -6.0, 6.0)
    return apply_scales(scale_key, base_field).astype(jnp.bfloat16)


def draw_centroids(key, part):
    key = jax.random.fold_in(key, 23)
    base_key, scale_key = jax.random.split(key)
    full_shape = (TILE, NTILES, D)
    base_field = jnp.clip(jax.random.normal(base_key, full_shape, jnp.float32), -6.0, 6.0)
    return apply_scales(scale_key, base_field).astype(jnp.bfloat16)


def member_plan(key):
    shard_count = N_SHARD
    device_count = N_GRP * N_SHARD
    per_cluster = SLOT // CL_DEV
    pool_size = shard_count * SLOT
    offset_key, device_key, table_key = jax.random.split(key, 3)
    offset = jax.random.randint(offset_key, (), 0, shard_count)
    devices_all = jnp.arange(device_count, dtype=jnp.int32)
    group_of = devices_all // shard_count
    shard_of = devices_all % shard_count
    hot_owner = (shard_of + offset) % shard_count
    entries = jnp.arange(pool_size, dtype=jnp.int32)
    entry_owner = entries // SLOT

    def one_device(dev_key, hot_id):
        rank_key, order_key = jax.random.split(dev_key)
        shuffled = jax.random.permutation(rank_key, pool_size).astype(jnp.int32)
        priority = shuffled + pool_size * (entry_owner != hot_id).astype(jnp.int32)
        ordering = jnp.argsort(priority)
        chosen = ordering[:PTS_DEV].astype(jnp.int32)
        return jax.random.permutation(order_key, chosen)
    picked = jax.vmap(one_device)(jax.random.split(device_key, device_count), hot_owner)
    owner_id = picked // SLOT
    within = picked % SLOT
    local_cluster = within % CL_DEV
    sub_index = within // CL_DEV
    cluster = (group_of[:, None] * shard_count + owner_id) * CL_DEV + local_cluster
    position = shard_of[:, None] * per_cluster + sub_index
    clusters_all = jnp.arange(CLUSTERS, dtype=jnp.int32)
    cluster_owner = clusters_all // CL_DEV % shard_count
    hot_sender = (cluster_owner - offset) % shard_count

    def one_table(cluster_key, sender_id):
        shuffled = jax.random.permutation(cluster_key, CAP).astype(jnp.int32)
        hot_pos = sender_id * per_cluster
        top_pos = jnp.argmax(shuffled == CAP - 1).astype(jnp.int32)
        moved = shuffled[hot_pos]
        shuffled = shuffled.at[top_pos].set(moved)
        return shuffled.at[hot_pos].set(CAP - 1)
    tables = jax.vmap(one_table)(jax.random.split(table_key, CLUSTERS), hot_sender)
    slot_value = tables[cluster, position]
    return (cluster.reshape(-1).astype(jnp.int32), slot_value.reshape(-1).astype(jnp.int32))


def draw_assign(key, part):
    return member_plan(key)[0]


def draw_slot_index(key, part):
    return member_plan(key)[1]


def set_ends(values, stream_key, low, top_value):
    extent = values.shape
    spot = [jax.random.randint(jax.random.fold_in(stream_key, axis), (), 0, extent[axis]) for axis in range(len(extent))]
    values = values.at[tuple(spot)].set(low)
    longest = extent.index(max(extent))
    spot[longest] = (spot[longest] + 1) % extent[longest]
    return values.at[tuple(spot)].set(top_value)


def rank_table(count, lean):
    portions = [(1 << 20) // math.isqrt(standing ** lean) + 1 for standing in range(1, count + 1)]
    width = 1 + sum(portions) // (1 << 30)
    return np.cumsum(np.array([max(1, weight // width) for weight in portions]))


def ranked(rng, shape, number_of, skew):
    grid = rank_table(number_of, skew)
    ticket = jax.random.randint(jax.random.fold_in(rng, 1), shape, 0, int(grid[number_of - 1]))
    grade = jnp.searchsorted(jnp.asarray(grid, jnp.int32), ticket, side="right")
    return jax.random.permutation(jax.random.fold_in(rng, 2), number_of)[grade].astype(jnp.int32)


def setup_inputs(seed: int = 0) -> dict:
    key_list = jax.random.split(jax.random.key(seed), 6)
    return {
        "points": draw_points(jax.random.fold_in(key_list[5], 71), 0),
        "centroids": draw_centroids(jax.random.fold_in(key_list[5], 71), 0),
        "candidates": set_ends(ranked(key_list[2], (NLISTS, K), NTILES, 2), jax.random.fold_in(key_list[2], 3), 0, NTILES - 1).astype(jnp.int32),
        "assign": draw_assign(jax.random.fold_in(key_list[5], 71), 0),
        "slot_index": draw_slot_index(jax.random.fold_in(key_list[5], 71), 0),
    }


eps = 1e-06
score_scale = 64.0

def inverse_norm(row_data):
    mean_square = lax.optimization_barrier(jnp.mean(jnp.square(row_data.astype(jnp.float32)), axis=-1))
    return lax.rsqrt(mean_square + eps) / math.sqrt(row_data.shape[-1])

def cluster_gram(cluster_rows, occupied):
    wide_rows = cluster_rows.astype(jnp.float32)
    inner_prod = jnp.einsum('cid,cjd->cij', wide_rows, wide_rows)
    unit_scale = inverse_norm(cluster_rows)
    gram_block = score_scale * inner_prod * unit_scale[:, :, None] * unit_scale[:, None, :]
    not_self = 1 - jnp.eye(CAP, dtype=jnp.int32) > 0
    others = (occupied[:, None, :] > 0) & not_self[None]
    highest = lax.optimization_barrier(jnp.max(jnp.where(others, gram_block, -jnp.inf), axis=2))
    best_row = jnp.where(jnp.any(others, axis=2), highest, 0.0)
    return (gram_block, best_row)

def reference(points, centroids, candidates, assign, slot_index):
    device_points = points.reshape(NLISTS, PTS_DEV, D)

    def list_scores(packed):
        point_rows, tile_ids = packed
        picked = jnp.take(centroids, tile_ids.astype(jnp.int32), axis=1)
        dots = jnp.einsum('id,rkd->ikr', point_rows.astype(jnp.float32), picked.astype(jnp.float32))
        column_scale = jnp.transpose(inverse_norm(picked))
        scaled = score_scale * dots * inverse_norm(point_rows)[:, None, None] * column_scale[None]
        return scaled.reshape(PTS_DEV, K * TILE)
    cand_scores = lax.map(list_scores, (device_points, candidates)).reshape(NPTS, K * TILE)
    per_group = N_SHARD * CL_DEV
    group_points = points.reshape(N_GRP, -1, D)
    group_assign = assign.reshape(N_GRP, -1)
    group_slots = slot_index.reshape(N_GRP, -1)

    def group_clusters(packed):
        group_id, these_points, these_assign, these_slots = packed
        local_row = ((these_assign - group_id * per_group) * CAP + these_slots).astype(jnp.int32)
        cluster_rows = jnp.zeros((per_group * CAP, D), jnp.bfloat16).at[local_row].set(these_points)
        occupied = jnp.zeros((per_group * CAP,), jnp.int32).at[local_row].set(1)
        gram_block, best_row = cluster_gram(cluster_rows.reshape(per_group, CAP, D), occupied.reshape(per_group, CAP))
        return (gram_block, best_row.reshape(-1)[local_row])
    group_ids = jnp.arange(N_GRP, dtype=jnp.int32)
    gram_all, best_all = lax.map(group_clusters, (group_ids, group_points, group_assign, group_slots))
    return (cand_scores, gram_all.reshape(CLUSTERS, CAP, CAP), best_all.reshape(NPTS))
```

```python
import functools

import jax
import jax.numpy as jnp
from jax import lax
from jax.experimental import pallas as pl
from jax.experimental.pallas import tpu as pltpu
from jax.sharding import PartitionSpec as P

D = 4096
TILE = 128
K = 2
CAP = 128
PTS = 256
CL = 4
NX, NY, NZ, NC = 4, 8, 12, 2
NS = NX * NY
NG = NZ * NC
TPG = 7
EPS = 1e-06
SCALE = 64.0
Q = 4
DQ = D // Q
DH = D // 2
MESH = pl.DeviceIdType.MESH
HI = lax.Precision.HIGHEST
F32 = jnp.float32
BF16 = jnp.bfloat16
I32 = jnp.int32
NT = (((1,), (1,)), ((), ()))


def iota(shape, dim):
    return lax.broadcasted_iota(I32, shape, dim)


def flag(cond, dtype=F32):
    return jnp.where(cond, 1.0, 0.0).astype(dtype)


def unit(total):
    return lax.rsqrt(total * (1.0 / D) + EPS) * (1.0 / 64.0)


def to_column(row):
    n = row.shape[1]
    return jnp.sum(jnp.where(iota((n, n), 0) == iota((n, n), 1), row, 0), axis=1, keepdims=True)


def to_row(column):
    n = column.shape[0]
    return jnp.sum(jnp.where(iota((n, n), 0) == iota((n, n), 1), column, 0), axis=0, keepdims=True)


def zigzag(i, n):
    return lax.rem(jnp.where(lax.rem(i, 2) == 1, (i + 1) // 2, n - i // 2), n)


def kernel(
    pts, cen, cand, asg, slt,
    out_scores, out_gram, out_best,
    send, got, tiles, csend, cgot, idsend, idgot, repsend, repgot,
    ps, pr, ids_s, ids_r, zs, zr, ks, cs, cr, rs, rr,
):
    grp, me = lax.axis_index("grp"), lax.axis_index("shard")
    z, core = grp // NC, lax.rem(grp, NC)
    x, y = me // NY, lax.rem(me, NY)

    def peer(k):
        xx = lax.rem(x + zigzag(k // NY, NX), NX)
        yy = lax.rem(y + zigzag(lax.rem(k, NY), NY), NY)
        return xx * NY + yy

    up = lax.rem(z + 1, NZ) * NC + core
    down = lax.rem(z + NZ - 1, NZ) * NC + core
    twin = z * NC + (1 - core)

    barrier = pltpu.get_barrier_semaphore()

    @pl.loop(1, NS)
    def _(k):
        pl.semaphore_signal(barrier, 1, device_id=(grp, peer(k)), device_id_type=MESH)

    for g in (up, down, twin):
        pl.semaphore_signal(barrier, 1, device_id=(g, me), device_id_type=MESH)
    pl.semaphore_wait(barrier, NS - 1 + 3)

    def tile_copy(entry, dest, ssem):
        return pltpu.make_async_remote_copy(
            src_ref=tiles.at[entry], dst_ref=tiles.at[entry], send_sem=ssem,
            recv_sem=zr.at[entry], device_id=(dest, me), device_id_type=MESH,
        )

    tiles[grp] = cen[...]
    tile_copy(grp, up, zs.at[0, 0]).start()
    tile_copy(grp, down, zs.at[1, 0]).start()
    tile_copy(grp, twin, ks.at[0, 0]).start()

    owner_row = lax.rem(asg[...] // CL, NS)
    member_row = lax.rem(asg[...], CL) * CAP + slt[...]
    own = flag(iota((NS, PTS), 0) == owner_row)
    before = flag(iota((PTS, PTS), 0) < iota((PTS, PTS), 1), BF16)
    ranks = jnp.dot(own.astype(BF16), before, preferred_element_type=F32)
    rank_row = jnp.sum(own * ranks, axis=0, keepdims=True).astype(I32)
    place_row = owner_row * 16 + rank_row
    at_rank = flag(iota((TILE, PTS), 0) == rank_row)

    ids = lax.dot_general(
        own * (member_row + 1).astype(F32), at_rank, NT, precision=HI, preferred_element_type=F32
    )
    ids = (ids + 0.5).astype(I32)
    for o in range(NS):
        idsend[o] = ids[o : o + 1]

    def quarter_slot(a, i):
        p = a * 16 + i
        quarter = (p >= 12).astype(I32) + (p >= 24).astype(I32) + (p >= 36).astype(I32)
        return quarter, p - 12 * quarter

    def point_copy(k):
        d = peer(k)
        return pltpu.make_async_remote_copy(
            src_ref=send.at[d], dst_ref=got.at[me], send_sem=ps.at[k], recv_sem=pr.at[me],
            device_id=(grp, d), device_id_type=MESH,
        )

    def id_copy(k):
        d = peer(k)
        return pltpu.make_async_remote_copy(
            src_ref=idsend.at[d], dst_ref=idgot.at[me], send_sem=ids_s.at[k], recv_sem=ids_r.at[me],
            device_id=(grp, d), device_id_type=MESH,
        )

    @pl.loop(0, NX)
    def _(j):
        xx = lax.rem(x + zigzag(j, NX), NX)
        line = iota((NY * 16, 1), 0)
        for a in range(3):
            quarter, slot = quarter_slot(a, lax.rem(line, 16))
            code = xx * (NY * 16) + line // 16 * 16 + slot
            total = None
            for q in (a, a + 1):
                pick = flag(jnp.where(quarter == q, code, -1) == place_row, BF16)
                part = jnp.dot(pick, pts[:, q * DQ : (q + 1) * DQ], preferred_element_type=F32)
                total = part if total is None else total + part
            send[pl.ds(xx * NY, NY), a * 16 : (a + 1) * 16, :] = total.astype(BF16).reshape(NY, 16, DQ)

        @pl.loop(jnp.where(j == 0, 1, 0), NY)
        def _(i):
            point_copy(j * NY + i).start()
            id_copy(j * NY + i).start()

    got[me] = send[me]
    idgot[me] = idsend[me]

    for step in range(1, NZ // 2 + 1):
        entry = lax.rem(z + NZ - step, NZ) * NC + core
        tile_copy(entry, up, zs.at[0, 0]).wait_recv()
        if step < NZ // 2:
            tile_copy(entry, up, zs.at[0, step]).start()
        tile_copy(entry, twin, ks.at[0, step]).start()
        if step < NZ // 2:
            entry = lax.rem(z + step, NZ) * NC + core
            tile_copy(entry, down, zs.at[0, 0]).wait_recv()
            if step < NZ // 2 - 1:
                tile_copy(entry, down, zs.at[1, step]).start()
            tile_copy(entry, twin, ks.at[1, step]).start()

    @pl.loop(0, NZ)
    def _(i):
        tile_copy(i * NC + 1 - core, twin, ks.at[0, 0]).wait_recv()

    line = iota((NS * 8, NS * K), 0)
    wanted = jnp.sum(
        jnp.where(line // 4 == iota((NS * 8, NS * K), 1), cand[...], 0), axis=1, keepdims=True
    )
    first = (wanted * 9363) >> 16
    code = first * 32 + lax.rem(iota((NS * 8, 1), 0), 4) * 8 + (wanted - first * TPG)
    pick = flag(code == iota((NS * 8, NG * 32), 1), BF16)

    @pl.loop(0, DH // 512)
    def _(i):
        halves = []
        for h in range(2):
            cols = pl.ds(pl.multiple_of(h * DH + i * 512, 512), 512)
            block = tiles[:, :, cols].reshape(NG * 32, 512)
            halves.append(jnp.dot(pick, block, preferred_element_type=F32).reshape(NS, 8, 512))
        both = jnp.concatenate(halves, axis=1).astype(BF16)
        csend[:, :, pl.ds(pl.multiple_of(i * 512, 512), 512)] = both

    def cen_copy(k):
        d = peer(k)
        return pltpu.make_async_remote_copy(
            src_ref=csend.at[d], dst_ref=cgot.at[me], send_sem=cs.at[k], recv_sem=cr.at[me],
            device_id=(grp, d), device_id_type=MESH,
        )

    @pl.loop(1, NS)
    def _(k):
        cen_copy(k).start()

    cgot[me] = csend[me]

    wide = pts[...].astype(F32)
    point_unit = unit(jnp.sum(wide * wide, axis=1, keepdims=True))

    def arrive(dst, sem, k):
        d = peer(k)
        pltpu.make_async_remote_copy(
            src_ref=dst.at[d], dst_ref=dst.at[d], send_sem=ps.at[0], recv_sem=sem.at[d],
            device_id=(grp, d), device_id_type=MESH,
        ).wait_recv()

    @pl.loop(1, NS)
    def _(k):
        arrive(idgot, ids_r, k)
        arrive(got, pr, k)

    idm = jnp.concatenate([idgot[o] for o in range(NS)], axis=0).astype(F32)
    lane = iota((1, NS * 16), 1)
    mine = iota((NS, NS * 16), 0) == iota((NS, NS * 16), 1) // 16

    def scatter(q, a):
        quarter, slot = quarter_slot(a, lax.rem(lane, 16))
        slot = jnp.where(quarter == q, slot, -1)
        spread = flag(iota((TILE, NS * 16), 0) == slot)
        ids = jnp.dot(idm, spread, precision=HI, preferred_element_type=F32)
        row = jnp.sum(jnp.where(mine, ids, 0.0), axis=0, keepdims=True)
        row = (row + 0.5).astype(I32)
        return iota((CL * CAP, NS * 16), 0) + 1 == row

    full = flag(scatter(0, 0))
    grams = [jnp.zeros((CAP, CAP), F32) for _ in range(CL)]
    for q in range(Q):
        maps = [(a, flag(scatter(q, a), BF16)) for a in (q - 1, q) if 0 <= a < 3]

        def step(i, acc):
            cols = pl.ds(pl.multiple_of(i * 256, 256), 256)
            rows = None
            for a, m in maps:
                block = got[:, a * 16 : (a + 1) * 16, cols].reshape(NS * 16, 256)
                part = jnp.dot(m, block, preferred_element_type=F32)
                rows = part if rows is None else rows + part
            rows = rows.astype(BF16)
            out = []
            for c in range(CL):
                r = rows[c * CAP : (c + 1) * CAP]
                out.append(acc[c] + lax.dot_general(r, r, NT, preferred_element_type=F32))
            return out

        grams = lax.fori_loop(0, DQ // 256, step, grams)

    occupied = jnp.sum(full, axis=1, keepdims=True)
    diagonal = iota((CAP, CAP), 0) == iota((CAP, CAP), 1)
    bests = []
    for c in range(CL):
        g = grams[c]
        d = jnp.where(diagonal, g, 0.0)
        u_col = unit(jnp.sum(d, axis=1, keepdims=True))
        u_row = unit(jnp.sum(d, axis=0, keepdims=True))
        g = SCALE * g * u_col * u_row
        out_gram[c] = g
        others = flag((occupied[c * CAP : (c + 1) * CAP] > 0.5) & jnp.logical_not(diagonal))
        best = jnp.max(jnp.where(others > 0.5, g, -jnp.inf), axis=0, keepdims=True)
        some = jnp.max(others, axis=0, keepdims=True) > 0.5
        bests.append(jnp.where(some, best, 0.0))
    best = jnp.concatenate(bests, axis=1)

    rep = jnp.dot(
        jnp.broadcast_to(best, (8, CL * CAP)), full, precision=HI, preferred_element_type=F32
    )[0:1]
    slots = flag(lax.rem(iota((NS * 16, TILE), 0), 16) == iota((NS * 16, TILE), 1))
    rep = jnp.dot(jnp.where(mine, rep, 0.0), slots, precision=HI, preferred_element_type=F32)
    for o in range(NS):
        repsend[o] = rep[o : o + 1]

    def rep_copy(k):
        d = peer(k)
        return pltpu.make_async_remote_copy(
            src_ref=repsend.at[d], dst_ref=repgot.at[me], send_sem=rs.at[k], recv_sem=rr.at[me],
            device_id=(grp, d), device_id_type=MESH,
        )

    @pl.loop(1, NS)
    def _(k):
        rep_copy(k).start()

    repgot[me] = repsend[me]

    @pl.loop(1, NS)
    def _(k):
        arrive(cgot, cr, k)

    line = iota((K * TILE, 1), 0)
    base = lax.rem(line, TILE) // 4 * 16 + line // TILE * 4 + lax.rem(line, 4)

    def score(i, acc):
        dots, squares = acc
        for h in range(2):
            perm = flag(base + h * 8 == iota((K * TILE, NS * 16), 1), BF16)
            block = cgot[:, :, pl.ds(pl.multiple_of(i * 512, 512), 512)].reshape(NS * 16, 512)
            rows = jnp.dot(perm, block, preferred_element_type=F32)
            squares = squares + jnp.sum(rows * rows, axis=1, keepdims=True)
            p = pts[:, pl.ds(pl.multiple_of(h * DH + i * 512, 512), 512)]
            dots = dots + lax.dot_general(p, rows.astype(BF16), NT, preferred_element_type=F32)
        return dots, squares

    dots, squares = lax.fori_loop(
        0, DH // 512, score, (jnp.zeros((PTS, K * TILE), F32), jnp.zeros((K * TILE, 1), F32))
    )
    out_scores[...] = SCALE * dots * point_unit * to_row(unit(squares))

    @pl.loop(1, NS)
    def _(k):
        arrive(repgot, rr, k)

    rep = jnp.concatenate([repgot[o] for o in range(NS)], axis=0)
    back = jnp.dot(rep, at_rank, precision=HI, preferred_element_type=F32)
    out_best[...] = jnp.sum(own * back, axis=0, keepdims=True)

    @pl.loop(1, NS)
    def _(k):
        point_copy(k).wait_send()
        id_copy(k).wait_send()
        cen_copy(k).wait_send()
        rep_copy(k).wait_send()

    tile_copy(grp, twin, ks.at[0, 0]).wait_send()
    for step in range(NZ // 2 + 1):
        if step < NZ // 2:
            tile_copy(grp, up, zs.at[0, step]).wait_send()
        if step < NZ // 2 - 1:
            tile_copy(grp, down, zs.at[1, step]).wait_send()
        if step > 0:
            tile_copy(grp, twin, ks.at[0, step]).wait_send()
        if 0 < step < NZ // 2:
            tile_copy(grp, twin, ks.at[1, step]).wait_send()


def on_device(points, centroids, candidates, assign, slot_index):
    cen = jnp.pad(centroids, ((0, 0), (0, 1), (0, 0))).reshape(4 * 8, D)
    dma = pltpu.SemaphoreType.DMA
    vmem = pl.BlockSpec(memory_space=pltpu.VMEM)
    scores, gram, best = pl.pallas_call(
        kernel,
        out_shape=(
            jax.ShapeDtypeStruct((PTS, K * TILE), F32),
            jax.ShapeDtypeStruct((CL, CAP, CAP), F32),
            jax.ShapeDtypeStruct((1, PTS), F32),
        ),
        in_specs=[vmem] * 5,
        out_specs=(vmem, vmem, vmem),
        scratch_shapes=[
            pltpu.VMEM((NS, 48, DQ), BF16),
            pltpu.VMEM((NS, 48, DQ), BF16),
            pltpu.VMEM((NG, 32, D), BF16),
            pltpu.VMEM((NS, 16, DH), BF16),
            pltpu.VMEM((NS, 16, DH), BF16),
            pltpu.VMEM((NS, 1, TILE), I32),
            pltpu.VMEM((NS, 1, TILE), I32),
            pltpu.VMEM((NS, 1, TILE), F32),
            pltpu.VMEM((NS, 1, TILE), F32),
            dma((NS,)), dma((NS,)), dma((NS,)), dma((NS,)),
            dma((2, NZ // 2)), dma((NG,)), dma((2, NZ // 2 + 1)),
            dma((NS,)), dma((NS,)), dma((NS,)), dma((NS,)),
        ],
        compiler_params=pltpu.CompilerParams(
            collective_id=0, has_side_effects=True, vmem_limit_bytes=56 << 20
        ),
        name="fused",
    )(
        points, cen, candidates.reshape(1, NS * K), assign.reshape(1, PTS),
        slot_index.reshape(1, PTS),
    )
    return scores, gram, best.reshape(PTS)


def solution(mesh):
    in_specs = (
        P(("grp", "shard"), None),
        P("shard", "grp", None),
        P("grp", None),
        P(("grp", "shard")),
        P(("grp", "shard")),
    )
    out_specs = (P(("grp", "shard"), None), P(("grp", "shard"), None, None), P(("grp", "shard")))
    return jax.shard_map(
        on_device, mesh=mesh, in_specs=in_specs, out_specs=out_specs, check_vma=False
    )
```

```python
import functools

import jax
import jax.numpy as jnp
from jax import lax
from jax.experimental import pallas as pl
from jax.experimental.pallas import tpu as pltpu
from jax.sharding import PartitionSpec as P

D = 4096
TILE = 128
K = 2
CAP = 128
PTS = 256
CL = 4
NX, NY, NZ, NC = 4, 8, 12, 2
NS = NX * NY
NG = NZ * NC
TPG = 7
EPS = 1e-06
SCALE = 64.0
Q = 4
DQ = D // Q
DH = D // 2
MESH = pl.DeviceIdType.MESH
HI = lax.Precision.HIGHEST
F32 = jnp.float32
BF16 = jnp.bfloat16
I32 = jnp.int32
NT = (((1,), (1,)), ((), ()))


def iota(shape, dim):
    return lax.broadcasted_iota(I32, shape, dim)


def flag(cond, dtype=F32):
    return jnp.where(cond, 1.0, 0.0).astype(dtype)


def unit(total):
    return lax.rsqrt(total * (1.0 / D) + EPS) * (1.0 / 64.0)


def to_row(column):
    n = column.shape[0]
    return jnp.sum(jnp.where(iota((n, n), 0) == iota((n, n), 1), column, 0), axis=0, keepdims=True)


def zigzag(i, n):
    return lax.rem(jnp.where(lax.rem(i, 2) == 1, (i + 1) // 2, n - i // 2), n)


def kernel(
    pts, cen, cand, asg, slt,
    out_scores, out_gram, out_best,
    send, got, tiles, csend, cgot, idsend, idgot, repsend, repgot,
    ps, pr, ids_s, ids_r, zs, zr, ks, cs, cr, rs, rr, token,
):
    grp, me = lax.axis_index("grp"), lax.axis_index("shard")
    z, core = grp // NC, lax.rem(grp, NC)
    x, y = me // NY, lax.rem(me, NY)

    def peer(k):
        xx = lax.rem(x + zigzag(k // NY, NX), NX)
        yy = lax.rem(y + zigzag(lax.rem(k, NY), NY), NY)
        return xx * NY + yy

    up = lax.rem(z + 1, NZ) * NC + core
    down = lax.rem(z + NZ - 1, NZ) * NC + core
    twin = z * NC + (1 - core)
    low, high = z == 0, z == NZ - 1

    barrier = pltpu.get_barrier_semaphore()

    @pl.loop(1, NS)
    def _(k):
        pl.semaphore_signal(barrier, 1, device_id=(grp, peer(k)), device_id_type=MESH)

    pl.semaphore_signal(barrier, 1, device_id=(twin, me), device_id_type=MESH)

    @pl.when(jnp.logical_not(high))
    def _():
        pl.semaphore_signal(barrier, 1, device_id=(up, me), device_id_type=MESH)

    @pl.when(jnp.logical_not(low))
    def _():
        pl.semaphore_signal(barrier, 1, device_id=(down, me), device_id_type=MESH)

    def tile_copy(entry, dest, ssem):
        return pltpu.make_async_remote_copy(
            src_ref=tiles.at[entry], dst_ref=tiles.at[entry], send_sem=ssem,
            recv_sem=zr.at[entry], device_id=(dest, me), device_id_type=MESH,
        )

    mine = [cen[t].astype(F32) for t in range(TPG)] + [jnp.zeros((4, D), F32)]
    tiles[grp] = jnp.concatenate(mine, axis=0).astype(BF16)

    owner_row = lax.rem(asg[...] // CL, NS)
    member_row = lax.rem(asg[...], CL) * CAP + slt[...]
    own = flag(iota((NS, PTS), 0) == owner_row)
    before = flag(iota((PTS, PTS), 0) < iota((PTS, PTS), 1), BF16)
    ranks = jnp.dot(own.astype(BF16), before, preferred_element_type=F32)
    rank_row = jnp.sum(own * ranks, axis=0, keepdims=True).astype(I32)
    place_row = owner_row * 16 + rank_row
    at_rank = flag(iota((TILE, PTS), 0) == rank_row)

    def quarter_slot(a, i):
        p = a * 16 + i
        quarter = (p >= 12).astype(I32) + (p >= 24).astype(I32) + (p >= 36).astype(I32)
        return quarter, p - 12 * quarter

    def point_copy(k):
        d = peer(k)
        return pltpu.make_async_remote_copy(
            src_ref=send.at[d], dst_ref=got.at[me], send_sem=ps.at[k], recv_sem=pr.at[me],
            device_id=(grp, d), device_id_type=MESH,
        )

    def id_copy(k):
        d = peer(k)
        return pltpu.make_async_remote_copy(
            src_ref=idsend.at[d], dst_ref=idgot.at[me], send_sem=ids_s.at[k], recv_sem=ids_r.at[me],
            device_id=(grp, d), device_id_type=MESH,
        )

    def build(j):
        xx = lax.rem(x + zigzag(j, NX), NX)
        line = iota((NY * 16, 1), 0)
        for a in range(3):
            quarter, slot = quarter_slot(a, lax.rem(line, 16))
            code = xx * (NY * 16) + line // 16 * 16 + slot
            total = None
            for q in (a, a + 1):
                pick = flag(jnp.where(quarter == q, code, -1) == place_row, BF16)
                part = jnp.dot(pick, pts[:, q * DQ : (q + 1) * DQ], preferred_element_type=F32)
                total = part if total is None else total + part
            send[pl.ds(xx * NY, NY), a * 16 : (a + 1) * 16, :] = total.astype(BF16).reshape(NY, 16, DQ)

    build(0)
    ends = low.astype(I32) + high.astype(I32)
    pl.semaphore_wait(barrier, NS - 1 + 3 - ends)

    @pl.when(low)
    def _():
        pl.semaphore_signal(token.at[0], 1, device_id=(up, me), device_id_type=MESH)

    @pl.when(high)
    def _():
        pl.semaphore_signal(token.at[1], 1, device_id=(down, me), device_id_type=MESH)

    @pl.when(jnp.logical_not(high))
    def _():
        tile_copy(grp, up, zs.at[0, 0]).start()

    @pl.when(jnp.logical_not(low))
    def _():
        tile_copy(grp, down, zs.at[1, 0]).start()

    tile_copy(grp, twin, ks.at[0, 0]).start()

    @pl.loop(0, NX)
    def _(j):
        @pl.loop(jnp.where(j == 0, 1, 0), NY)
        def _(i):
            point_copy(j * NY + i).start()

        @pl.when(j < NX - 1)
        def _():
            build(j + 1)

    ids = lax.dot_general(
        own * (member_row + 1).astype(F32), at_rank, NT, precision=HI, preferred_element_type=F32
    )
    ids = (ids + 0.5).astype(I32)
    for o in range(NS):
        idsend[o] = ids[o : o + 1]

    @pl.loop(1, NS)
    def _(k):
        id_copy(k).start()

    got[me] = send[me]
    idgot[me] = idsend[me]

    @pl.when(jnp.logical_not(low))
    def _():
        pl.semaphore_wait(token.at[0], 1)

        @pl.when(jnp.logical_not(high))
        def _():
            pl.semaphore_signal(token.at[0], 1, device_id=(up, me), device_id_type=MESH)

    @pl.when(jnp.logical_not(high))
    def _():
        pl.semaphore_wait(token.at[1], 1)

        @pl.when(jnp.logical_not(low))
        def _():
            pl.semaphore_signal(token.at[1], 1, device_id=(down, me), device_id_type=MESH)

    @pl.when(high)
    def _():
        tile_copy(grp, up, zs.at[0, 0]).start()

    @pl.when(low)
    def _():
        tile_copy(grp, down, zs.at[1, 0]).start()

    for step in range(1, NZ // 2 + 1):
        entry = lax.rem(z + NZ - step, NZ) * NC + core
        tile_copy(entry, up, zs.at[0, 0]).wait_recv()
        if step < NZ // 2:
            tile_copy(entry, up, zs.at[0, step]).start()
        tile_copy(entry, twin, ks.at[0, step]).start()
        if step < NZ // 2:
            entry = lax.rem(z + step, NZ) * NC + core
            tile_copy(entry, down, zs.at[0, 0]).wait_recv()
            if step < NZ // 2 - 1:
                tile_copy(entry, down, zs.at[1, step]).start()
            tile_copy(entry, twin, ks.at[1, step]).start()

    @pl.loop(0, NZ)
    def _(i):
        tile_copy(i * NC + 1 - core, twin, ks.at[0, 0]).wait_recv()

    line = iota((NS * 8, NS), 0)
    wanted = jnp.zeros((NS * 8, 1), I32)
    for k in range(K):
        here = line // 4 == iota((NS * 8, NS), 1) * K + k
        wanted += jnp.sum(jnp.where(here, cand[k : k + 1], 0), axis=1, keepdims=True)
    first = (wanted * 9363) >> 16
    code = first * 32 + (wanted - first * TPG) * 4 + lax.rem(iota((NS * 8, 1), 0), 4)
    pick = flag(code == iota((NS * 8, NG * 32), 1), BF16)

    @pl.loop(0, DH // 512)
    def _(i):
        halves = []
        for h in range(2):
            cols = pl.ds(pl.multiple_of(h * DH + i * 512, 512), 512)
            block = tiles[:, :, cols].reshape(NG * 32, 512)
            halves.append(jnp.dot(pick, block, preferred_element_type=F32).reshape(NS, 8, 512))
        both = jnp.concatenate(halves, axis=1).astype(BF16)
        csend[:, :, pl.ds(pl.multiple_of(i * 512, 512), 512)] = both

    def cen_copy(k):
        d = peer(k)
        return pltpu.make_async_remote_copy(
            src_ref=csend.at[d], dst_ref=cgot.at[me], send_sem=cs.at[k], recv_sem=cr.at[me],
            device_id=(grp, d), device_id_type=MESH,
        )

    @pl.loop(1, NS)
    def _(k):
        cen_copy(k).start()

    cgot[me] = csend[me]

    wide = pts[...].astype(F32)
    point_unit = unit(jnp.sum(wide * wide, axis=1, keepdims=True))

    def arrive(dst, sem, d):
        pltpu.make_async_remote_copy(
            src_ref=dst.at[d], dst_ref=dst.at[d], send_sem=ps.at[0], recv_sem=sem.at[d],
            device_id=(grp, d), device_id_type=MESH,
        ).wait_recv()

    @pl.loop(1, NS)
    def _(k):
        arrive(idgot, ids_r, peer(k))
        arrive(got, pr, peer(k))

    idm = jnp.concatenate([idgot[o] for o in range(NS)], axis=0).astype(F32)
    lane = iota((1, NS * 16), 1)
    mine = iota((NS, NS * 16), 0) == iota((NS, NS * 16), 1) // 16

    def scatter(q, a):
        quarter, slot = quarter_slot(a, lax.rem(lane, 16))
        slot = jnp.where(quarter == q, slot, -1)
        spread = flag(iota((TILE, NS * 16), 0) == slot)
        ids = jnp.dot(idm, spread, precision=HI, preferred_element_type=F32)
        row = jnp.sum(jnp.where(mine, ids, 0.0), axis=0, keepdims=True)
        row = (row + 0.5).astype(I32)
        return iota((CL * CAP, NS * 16), 0) + 1 == row

    full = flag(scatter(0, 0))
    grams = [jnp.zeros((CAP, CAP), F32) for _ in range(CL)]
    for q in range(Q):
        maps = [(a, flag(scatter(q, a), BF16)) for a in (q - 1, q) if 0 <= a < 3]

        def step(i, acc):
            cols = pl.ds(pl.multiple_of(i * 256, 256), 256)
            rows = None
            for a, m in maps:
                block = got[:, a * 16 : (a + 1) * 16, cols].reshape(NS * 16, 256)
                part = jnp.dot(m, block, preferred_element_type=F32)
                rows = part if rows is None else rows + part
            rows = rows.astype(BF16)
            out = []
            for c in range(CL):
                r = rows[c * CAP : (c + 1) * CAP]
                out.append(acc[c] + lax.dot_general(r, r, NT, preferred_element_type=F32))
            return out

        grams = lax.fori_loop(0, DQ // 256, step, grams)

    occupied = jnp.sum(full, axis=1, keepdims=True)
    diagonal = iota((CAP, CAP), 0) == iota((CAP, CAP), 1)
    bests = []
    for c in range(CL):
        g = grams[c]
        d = jnp.where(diagonal, g, 0.0)
        u_col = unit(jnp.sum(d, axis=1, keepdims=True))
        u_row = unit(jnp.sum(d, axis=0, keepdims=True))
        g = SCALE * g * u_col * u_row
        out_gram[c] = g
        others = flag((occupied[c * CAP : (c + 1) * CAP] > 0.5) & jnp.logical_not(diagonal))
        best = jnp.max(jnp.where(others > 0.5, g, -jnp.inf), axis=0, keepdims=True)
        some = jnp.max(others, axis=0, keepdims=True) > 0.5
        bests.append(jnp.where(some, best, 0.0))
    best = jnp.concatenate(bests, axis=1)

    rep = jnp.dot(
        jnp.broadcast_to(best, (8, CL * CAP)), full, precision=HI, preferred_element_type=F32
    )[0:1]
    slots = flag(lax.rem(iota((NS * 16, TILE), 0), 16) == iota((NS * 16, TILE), 1))
    rep = jnp.dot(jnp.where(mine, rep, 0.0), slots, precision=HI, preferred_element_type=F32)
    for o in range(NS):
        repsend[o] = rep[o : o + 1]

    def rep_copy(k):
        d = peer(k)
        return pltpu.make_async_remote_copy(
            src_ref=repsend.at[d], dst_ref=repgot.at[me], send_sem=rs.at[k], recv_sem=rr.at[me],
            device_id=(grp, d), device_id_type=MESH,
        )

    @pl.loop(1, NS)
    def _(k):
        rep_copy(k).start()

    repgot[me] = repsend[me]

    out_scores[...] = jnp.zeros((PTS, K * TILE), F32)
    line = iota((NY * 8, 1), 0)
    base = lax.rem(line, NY * 4) // 4 * 16 + line // (NY * 4) * 4 + lax.rem(line, 4)
    column = line // (NY * 4) * TILE + lax.rem(line, NY * 4)

    @pl.loop(0, NX)
    def _(j):
        xx = lax.rem(x - zigzag(j, NX) + NX, NX)

        @pl.loop(jnp.where(j == 0, 1, 0), NY)
        def _(i):
            arrive(cgot, cr, xx * NY + lax.rem(y - zigzag(i, NY) + NY, NY))

        def score(i, acc):
            dots, squares = acc
            for h in range(2):
                perm = flag(base + h * 8 == iota((NY * 8, NY * 16), 1), BF16)
                cols = pl.ds(pl.multiple_of(i * 512, 512), 512)
                block = cgot[pl.ds(xx * NY, NY), :, cols].reshape(NY * 16, 512)
                rows = jnp.dot(perm, block, preferred_element_type=F32)
                squares = squares + jnp.sum(rows * rows, axis=1, keepdims=True)
                p = pts[:, pl.ds(pl.multiple_of(h * DH + i * 512, 512), 512)]
                dots = dots + lax.dot_general(p, rows.astype(BF16), NT, preferred_element_type=F32)
            return dots, squares

        dots, squares = lax.fori_loop(
            0, DH // 512, score, (jnp.zeros((PTS, NY * 8), F32), jnp.zeros((NY * 8, 1), F32))
        )
        put = flag(column + xx * (NY * 4) == iota((NY * 8, K * TILE), 1))
        dots = SCALE * dots * point_unit * to_row(unit(squares))
        out_scores[...] += jnp.dot(dots, put, precision=HI, preferred_element_type=F32)

    @pl.loop(1, NS)
    def _(k):
        arrive(repgot, rr, peer(k))

    rep = jnp.concatenate([repgot[o] for o in range(NS)], axis=0)
    back = jnp.dot(rep, at_rank, precision=HI, preferred_element_type=F32)
    out_best[...] = jnp.sum(own * back, axis=0, keepdims=True)

    @pl.loop(1, NS)
    def _(k):
        point_copy(k).wait_send()
        id_copy(k).wait_send()
        cen_copy(k).wait_send()
        rep_copy(k).wait_send()

    tile_copy(grp, twin, ks.at[0, 0]).wait_send()
    for step in range(NZ // 2 + 1):
        if step < NZ // 2:
            tile_copy(grp, up, zs.at[0, step]).wait_send()
        if step < NZ // 2 - 1:
            tile_copy(grp, down, zs.at[1, step]).wait_send()
        if step > 0:
            tile_copy(grp, twin, ks.at[0, step]).wait_send()
        if 0 < step < NZ // 2:
            tile_copy(grp, twin, ks.at[1, step]).wait_send()


def deliver(a, b, c, out_a, out_b, out_c):
    out_a[...] = a[...]
    out_b[...] = b[...]
    out_c[...] = c[...]


def on_device(points, centroids, candidates, assign, slot_index):
    cen = jnp.transpose(centroids, (1, 0, 2))
    dma = pltpu.SemaphoreType.DMA
    vmem = pl.BlockSpec(memory_space=pltpu.VMEM)
    outs = pl.pallas_call(
        kernel,
        out_shape=(
            jax.ShapeDtypeStruct((PTS, K * TILE), F32),
            jax.ShapeDtypeStruct((CL, CAP, CAP), F32),
            jax.ShapeDtypeStruct((1, PTS), F32),
        ),
        in_specs=[vmem] * 5,
        out_specs=(vmem, vmem, vmem),
        scratch_shapes=[
            pltpu.VMEM((NS, 48, DQ), BF16),
            pltpu.VMEM((NS, 48, DQ), BF16),
            pltpu.VMEM((NG, 32, D), BF16),
            pltpu.VMEM((NS, 16, DH), BF16),
            pltpu.VMEM((NS, 16, DH), BF16),
            pltpu.VMEM((NS, 1, TILE), I32),
            pltpu.VMEM((NS, 1, TILE), I32),
            pltpu.VMEM((NS, 1, TILE), F32),
            pltpu.VMEM((NS, 1, TILE), F32),
            dma((NS,)), dma((NS,)), dma((NS,)), dma((NS,)),
            dma((2, NZ // 2)), dma((NG,)), dma((2, NZ // 2 + 1)),
            dma((NS,)), dma((NS,)), dma((NS,)), dma((NS,)),
            pltpu.SemaphoreType.REGULAR((2,)),
        ],
        compiler_params=pltpu.CompilerParams(
            collective_id=0, has_side_effects=True, vmem_limit_bytes=56 << 20
        ),
        name="fused",
    )(
        points, cen, candidates.T, assign.reshape(1, PTS),
        slot_index.reshape(1, PTS),
    )
    scores, gram, best = pl.pallas_call(
        deliver,
        out_shape=tuple(jax.ShapeDtypeStruct(o.shape, o.dtype) for o in outs),
        in_specs=[vmem] * 3,
        out_specs=(vmem,) * 3,
        compiler_params=pltpu.CompilerParams(vmem_limit_bytes=56 << 20),
        name="deliver",
    )(*outs)
    return scores, gram, best.reshape(PTS)


def solution(mesh):
    in_specs = (
        P(("grp", "shard"), None),
        P("shard", "grp", None),
        P("grp", None),
        P(("grp", "shard")),
        P(("grp", "shard")),
    )
    out_specs = (P(("grp", "shard"), None), P(("grp", "shard"), None, None), P(("grp", "shard")))
    return jax.shard_map(
        on_device, mesh=mesh, in_specs=in_specs, out_specs=out_specs, check_vma=False
    )
```

```python
import functools

import jax
import jax.numpy as jnp
from jax import lax
from jax.experimental import pallas as pl
from jax.experimental.pallas import tpu as pltpu
from jax.sharding import PartitionSpec as P

D = 4096
TILE = 128
K = 2
CAP = 128
PTS = 256
CL = 4
NX, NY, NZ, NC = 4, 8, 12, 2
NS = NX * NY
NG = NZ * NC
TPG = 7
EPS = 1e-06
SCALE = 64.0
Q = 4
DQ = D // Q
DH = D // 2
MESH = pl.DeviceIdType.MESH
HI = lax.Precision.HIGHEST
F32 = jnp.float32
BF16 = jnp.bfloat16
I32 = jnp.int32
NT = (((1,), (1,)), ((), ()))


def iota(shape, dim):
    return lax.broadcasted_iota(I32, shape, dim)


def flag(cond, dtype=F32):
    return jnp.where(cond, 1.0, 0.0).astype(dtype)


def unit(total):
    return lax.rsqrt(total * (1.0 / D) + EPS) * (1.0 / 64.0)


def to_row(column):
    n = column.shape[0]
    return jnp.sum(jnp.where(iota((n, n), 0) == iota((n, n), 1), column, 0), axis=0, keepdims=True)


def zigzag(i, n):
    return lax.rem(jnp.where(lax.rem(i, 2) == 1, (i + 1) // 2, n - i // 2), n)


def kernel(
    pts, cen, cand, asg, slt,
    out_scores, out_gram, out_best,
    send, got, tiles, csend, cgot, idsend, idgot, repsend, repgot,
    ps, pr, ids_s, ids_r, zs, zr, ks, cs, cr, rs, rr, token, xs,
):
    grp, me = lax.axis_index("grp"), lax.axis_index("shard")
    z, core = grp // NC, lax.rem(grp, NC)
    x, y = me // NY, lax.rem(me, NY)

    def peer(k):
        xx = lax.rem(x + zigzag(k // NY, NX), NX)
        yy = lax.rem(y + zigzag(lax.rem(k, NY), NY), NY)
        return xx * NY + yy

    up = lax.rem(z + 1, NZ) * NC + core
    down = lax.rem(z + NZ - 1, NZ) * NC + core
    twin = z * NC + (1 - core)
    low, high = z == 0, z == NZ - 1

    barrier = pltpu.get_barrier_semaphore()

    @pl.loop(1, NS)
    def _(k):
        pl.semaphore_signal(barrier, 1, device_id=(grp, peer(k)), device_id_type=MESH)

    pl.semaphore_signal(barrier, 1, device_id=(twin, me), device_id_type=MESH)

    @pl.when(jnp.logical_not(high))
    def _():
        pl.semaphore_signal(barrier, 1, device_id=(up, me), device_id_type=MESH)

    @pl.when(jnp.logical_not(low))
    def _():
        pl.semaphore_signal(barrier, 1, device_id=(down, me), device_id_type=MESH)

    across = x * NY + lax.rem(y + NY // 2, NY)

    def tile_copy(part, entry, dest, ssem):
        return pltpu.make_async_remote_copy(
            src_ref=tiles.at[part, entry], dst_ref=tiles.at[part, entry], send_sem=ssem,
            recv_sem=zr.at[part, entry], device_id=(dest, me), device_id_type=MESH,
        )

    swap = pltpu.make_async_remote_copy(
        src_ref=tiles.at[0, grp], dst_ref=tiles.at[1, grp], send_sem=xs.at[0],
        recv_sem=zr.at[1, grp], device_id=(grp, across), device_id_type=MESH,
    )

    mine = [cen[t].astype(F32) for t in range(TPG)] + [jnp.zeros((4, D), F32)]
    tiles[0, grp] = jnp.concatenate(mine, axis=0).astype(BF16)

    owner_row = lax.rem(asg[...] // CL, NS)
    member_row = lax.rem(asg[...], CL) * CAP + slt[...]
    own = flag(iota((NS, PTS), 0) == owner_row)
    before = flag(iota((PTS, PTS), 0) < iota((PTS, PTS), 1), BF16)
    ranks = jnp.dot(own.astype(BF16), before, preferred_element_type=F32)
    rank_row = jnp.sum(own * ranks, axis=0, keepdims=True).astype(I32)
    place_row = owner_row * 16 + rank_row
    at_rank = flag(iota((TILE, PTS), 0) == rank_row)

    def quarter_slot(a, i):
        p = a * 16 + i
        quarter = (p >= 12).astype(I32) + (p >= 24).astype(I32) + (p >= 36).astype(I32)
        return quarter, p - 12 * quarter

    def point_copy(k):
        d = peer(k)
        return pltpu.make_async_remote_copy(
            src_ref=send.at[d], dst_ref=got.at[me], send_sem=ps.at[k], recv_sem=pr.at[me],
            device_id=(grp, d), device_id_type=MESH,
        )

    def id_copy(k):
        d = peer(k)
        return pltpu.make_async_remote_copy(
            src_ref=idsend.at[d], dst_ref=idgot.at[me], send_sem=ids_s.at[k], recv_sem=ids_r.at[me],
            device_id=(grp, d), device_id_type=MESH,
        )

    def build(j):
        xx = lax.rem(x + zigzag(j, NX), NX)
        line = iota((NY * 16, 1), 0)
        for a in range(3):
            quarter, slot = quarter_slot(a, lax.rem(line, 16))
            code = xx * (NY * 16) + line // 16 * 16 + slot
            total = None
            for q in (a, a + 1):
                pick = flag(jnp.where(quarter == q, code, -1) == place_row, BF16)
                part = jnp.dot(pick, pts[:, q * DQ : (q + 1) * DQ], preferred_element_type=F32)
                total = part if total is None else total + part
            send[pl.ds(xx * NY, NY), a * 16 : (a + 1) * 16, :] = total.astype(BF16).reshape(NY, 16, DQ)

    build(0)
    ends = low.astype(I32) + high.astype(I32)
    pl.semaphore_wait(barrier, NS - 1 + 3 - ends)

    @pl.when(low)
    def _():
        pl.semaphore_signal(token.at[0], 1, device_id=(up, me), device_id_type=MESH)

    @pl.when(high)
    def _():
        pl.semaphore_signal(token.at[1], 1, device_id=(down, me), device_id_type=MESH)

    swap.start()

    def own_tiles(part):
        @pl.when(jnp.logical_not(high))
        def _():
            tile_copy(part, grp, up, zs.at[part, 0, 0]).start()

        @pl.when(jnp.logical_not(low))
        def _():
            tile_copy(part, grp, down, zs.at[part, 1, 0]).start()

        tile_copy(part, grp, twin, ks.at[part, 0, 0]).start()

    own_tiles(0)

    @pl.loop(0, NX)
    def _(j):
        @pl.loop(jnp.where(j == 0, 1, 0), NY)
        def _(i):
            point_copy(j * NY + i).start()

        @pl.when(j < NX - 1)
        def _():
            build(j + 1)

    ids = lax.dot_general(
        own * (member_row + 1).astype(F32), at_rank, NT, precision=HI, preferred_element_type=F32
    )
    ids = (ids + 0.5).astype(I32)
    for o in range(NS):
        idsend[o] = ids[o : o + 1]

    @pl.loop(1, NS)
    def _(k):
        id_copy(k).start()

    got[me] = send[me]
    idgot[me] = idsend[me]

    def token_down():
        pl.semaphore_wait(token.at[1], 1)

        @pl.when(jnp.logical_not(low))
        def _():
            pl.semaphore_signal(token.at[1], 1, device_id=(down, me), device_id_type=MESH)

    @pl.when(jnp.logical_not(low))
    def _():
        pl.semaphore_wait(token.at[0], 1)

        @pl.when(jnp.logical_not(high))
        def _():
            pl.semaphore_signal(token.at[0], 1, device_id=(up, me), device_id_type=MESH)

    @pl.when((z >= NZ // 2) & (z < NZ - 1))
    def _():
        token_down()

    @pl.when(high)
    def _():
        tile_copy(0, grp, up, zs.at[0, 0, 0]).start()

    reach = ((NZ // 2, NZ // 2 - 1), (NZ // 2 - 1, NZ // 2))

    def forward(part, way, step):
        dest, shift = ((up, NZ - step), (down, step))[way]
        entry = lax.rem(z + shift, NZ) * NC + core
        tile_copy(part, entry, dest, zs.at[part, way, 0]).wait_recv()

        @pl.when(step < reach[part][way])
        def _():
            tile_copy(part, entry, dest, zs.at[part, way, step]).start()

        tile_copy(part, entry, twin, ks.at[part, way, step]).start()

    lags = ((0, 3), (2, 6))

    def turn(t):
        for part in range(2):
            for late in range(2):
                for way in range(2):
                    step = t - lags[part][late]
                    if (part, late, way) == (0, 0, 1):
                        step -= low.astype(I32)
                    inside = (z, NZ - 1 - z)[way]
                    due = step > inside if late else step <= inside

                    @pl.when(due & (step >= 1) & (step <= reach[part][way]))
                    def _():
                        forward(part, way, step)

    def near(i, count):
        xx = lax.rem(x + zigzag(i // count, NX), NX)
        return xx * NY + lax.rem(y + zigzag(lax.rem(i, count), NY), NY)

    def cen_copy(part, i):
        slot = (me, across)[part]
        d = near(i, (5, 3)[part])
        j = i + (0, 5 * NX)[part]
        return pltpu.make_async_remote_copy(
            src_ref=csend.at[j], dst_ref=cgot.at[slot], send_sem=cs.at[j], recv_sem=cr.at[slot],
            device_id=(grp, d), device_id_type=MESH,
        )

    def select(part):
        @pl.loop(0, NZ)
        def _(i):
            tile_copy(part, i * NC + 1 - core, twin, ks.at[part, 0, 0]).wait_recv()

        count = (5, 3)[part]
        n = count * NX
        line = iota((n * 8, NS), 0)
        dest = near(line // 8, count) == iota((n * 8, NS), 1)
        wanted = jnp.zeros((n * 8, 1), I32)
        for k in range(K):
            here = dest & (lax.rem(line, 8) // 4 == k)
            wanted += jnp.sum(jnp.where(here, cand[k : k + 1], 0), axis=1, keepdims=True)
        first = (wanted * 9363) >> 16
        code = first * 32 + (wanted - first * TPG) * 4 + lax.rem(iota((n * 8, 1), 0), 4)
        pick = flag(code == iota((n * 8, NG * 32), 1), BF16)
        start = (0, 5 * NX)[part]

        @pl.loop(0, DH // 512)
        def _(i):
            halves = []
            for h in range(2):
                cols = pl.ds(pl.multiple_of(h * DH + i * 512, 512), 512)
                block = tiles[part, :, :, cols].reshape(NG * 32, 512)
                halves.append(jnp.dot(pick, block, preferred_element_type=F32).reshape(n, 8, 512))
            both = jnp.concatenate(halves, axis=1).astype(BF16)
            csend[start : start + n, :, pl.ds(pl.multiple_of(i * 512, 512), 512)] = both

        @pl.loop(1, n)
        def _(i):
            cen_copy(part, i).start()

        cgot[(me, across)[part]] = csend[start]

    @pl.loop(1, 10)
    def _(t):
        turn(t)

        @pl.when(t == 1)
        def _():
            swap.wait_recv()
            own_tiles(1)

            @pl.when(high)
            def _():
                tile_copy(1, grp, up, zs.at[1, 0, 0]).start()

            @pl.when(z < NZ // 2)
            def _():
                token_down()

            @pl.when(low)
            def _():
                for part in range(2):
                    tile_copy(part, grp, down, zs.at[part, 1, 0]).start()

    select(0)

    @pl.loop(10, 13)
    def _(t):
        turn(t)

    select(1)

    wide = pts[...].astype(F32)
    point_unit = unit(jnp.sum(wide * wide, axis=1, keepdims=True))

    def arrive(dst, sem, d):
        pltpu.make_async_remote_copy(
            src_ref=dst.at[d], dst_ref=dst.at[d], send_sem=ps.at[0], recv_sem=sem.at[d],
            device_id=(grp, d), device_id_type=MESH,
        ).wait_recv()

    @pl.loop(1, NS)
    def _(k):
        arrive(idgot, ids_r, peer(k))
        arrive(got, pr, peer(k))

    idm = jnp.concatenate([idgot[o] for o in range(NS)], axis=0).astype(F32)
    lane = iota((1, NS * 16), 1)
    mine = iota((NS, NS * 16), 0) == iota((NS, NS * 16), 1) // 16

    def scatter(q, a):
        quarter, slot = quarter_slot(a, lax.rem(lane, 16))
        slot = jnp.where(quarter == q, slot, -1)
        spread = flag(iota((TILE, NS * 16), 0) == slot)
        ids = jnp.dot(idm, spread, precision=HI, preferred_element_type=F32)
        row = jnp.sum(jnp.where(mine, ids, 0.0), axis=0, keepdims=True)
        row = (row + 0.5).astype(I32)
        return iota((CL * CAP, NS * 16), 0) + 1 == row

    full = flag(scatter(0, 0))
    grams = [jnp.zeros((CAP, CAP), F32) for _ in range(CL)]
    for q in range(Q):
        maps = [(a, flag(scatter(q, a), BF16)) for a in (q - 1, q) if 0 <= a < 3]

        def step(i, acc):
            cols = pl.ds(pl.multiple_of(i * 256, 256), 256)
            rows = None
            for a, m in maps:
                block = got[:, a * 16 : (a + 1) * 16, cols].reshape(NS * 16, 256)
                part = jnp.dot(m, block, preferred_element_type=F32)
                rows = part if rows is None else rows + part
            rows = rows.astype(BF16)
            out = []
            for c in range(CL):
                r = rows[c * CAP : (c + 1) * CAP]
                out.append(acc[c] + lax.dot_general(r, r, NT, preferred_element_type=F32))
            return out

        grams = lax.fori_loop(0, DQ // 256, step, grams)

    occupied = jnp.sum(full, axis=1, keepdims=True)
    diagonal = iota((CAP, CAP), 0) == iota((CAP, CAP), 1)
    bests = []
    for c in range(CL):
        g = grams[c]
        d = jnp.where(diagonal, g, 0.0)
        u_col = unit(jnp.sum(d, axis=1, keepdims=True))
        u_row = unit(jnp.sum(d, axis=0, keepdims=True))
        g = SCALE * g * u_col * u_row
        out_gram[c] = g
        others = flag((occupied[c * CAP : (c + 1) * CAP] > 0.5) & jnp.logical_not(diagonal))
        best = jnp.max(jnp.where(others > 0.5, g, -jnp.inf), axis=0, keepdims=True)
        some = jnp.max(others, axis=0, keepdims=True) > 0.5
        bests.append(jnp.where(some, best, 0.0))
    best = jnp.concatenate(bests, axis=1)

    rep = jnp.dot(
        jnp.broadcast_to(best, (8, CL * CAP)), full, precision=HI, preferred_element_type=F32
    )[0:1]
    slots = flag(lax.rem(iota((NS * 16, TILE), 0), 16) == iota((NS * 16, TILE), 1))
    rep = jnp.dot(jnp.where(mine, rep, 0.0), slots, precision=HI, preferred_element_type=F32)
    for o in range(NS):
        repsend[o] = rep[o : o + 1]

    def rep_copy(k):
        d = peer(k)
        return pltpu.make_async_remote_copy(
            src_ref=repsend.at[d], dst_ref=repgot.at[me], send_sem=rs.at[k], recv_sem=rr.at[me],
            device_id=(grp, d), device_id_type=MESH,
        )

    @pl.loop(1, NS)
    def _(k):
        rep_copy(k).start()

    repgot[me] = repsend[me]

    out_scores[...] = jnp.zeros((PTS, K * TILE), F32)
    line = iota((NY * 8, 1), 0)
    base = lax.rem(line, NY * 4) // 4 * 16 + line // (NY * 4) * 4 + lax.rem(line, 4)
    column = line // (NY * 4) * TILE + lax.rem(line, NY * 4)

    @pl.loop(0, NX)
    def _(j):
        xx = lax.rem(x - zigzag(j, NX) + NX, NX)

        @pl.loop(jnp.where(j == 0, 1, 0), jnp.where(j == 0, NY - 1, NY))
        def _(i):
            arrive(cgot, cr, xx * NY + lax.rem(y - zigzag(i, NY) + NY, NY))

        def score(i, acc):
            dots, squares = acc
            for h in range(2):
                perm = flag(base + h * 8 == iota((NY * 8, NY * 16), 1), BF16)
                cols = pl.ds(pl.multiple_of(i * 512, 512), 512)
                block = cgot[pl.ds(xx * NY, NY), :, cols].reshape(NY * 16, 512)
                rows = jnp.dot(perm, block, preferred_element_type=F32)
                squares = squares + jnp.sum(rows * rows, axis=1, keepdims=True)
                p = pts[:, pl.ds(pl.multiple_of(h * DH + i * 512, 512), 512)]
                dots = dots + lax.dot_general(p, rows.astype(BF16), NT, preferred_element_type=F32)
            return dots, squares

        dots, squares = lax.fori_loop(
            0, DH // 512, score, (jnp.zeros((PTS, NY * 8), F32), jnp.zeros((NY * 8, 1), F32))
        )
        put = flag(column + xx * (NY * 4) == iota((NY * 8, K * TILE), 1))
        dots = SCALE * dots * point_unit * to_row(unit(squares))
        out_scores[...] += jnp.dot(dots, put, precision=HI, preferred_element_type=F32)

    @pl.loop(1, NS)
    def _(k):
        arrive(repgot, rr, peer(k))

    rep = jnp.concatenate([repgot[o] for o in range(NS)], axis=0)
    back = jnp.dot(rep, at_rank, precision=HI, preferred_element_type=F32)
    out_best[...] = jnp.sum(own * back, axis=0, keepdims=True)

    @pl.loop(1, NS)
    def _(k):
        point_copy(k).wait_send()
        id_copy(k).wait_send()
        rep_copy(k).wait_send()

    swap.wait_send()
    for part in range(2):

        @pl.loop(1, (5, 3)[part] * NX)
        def _(i):
            cen_copy(part, i).wait_send()

        tile_copy(part, grp, twin, ks.at[part, 0, 0]).wait_send()
        for way in range(2):
            for step in range(reach[part][way]):
                tile_copy(part, grp, up, zs.at[part, way, step]).wait_send()
                tile_copy(part, grp, twin, ks.at[part, way, step + 1]).wait_send()


def deliver(a, b, c, out_a, out_b, out_c):
    out_a[...] = a[...]
    out_b[...] = b[...]
    out_c[...] = c[...]


def on_device(points, centroids, candidates, assign, slot_index):
    cen = jnp.transpose(centroids, (1, 0, 2))
    dma = pltpu.SemaphoreType.DMA
    vmem = pl.BlockSpec(memory_space=pltpu.VMEM)
    outs = pl.pallas_call(
        kernel,
        out_shape=(
            jax.ShapeDtypeStruct((PTS, K * TILE), F32),
            jax.ShapeDtypeStruct((CL, CAP, CAP), F32),
            jax.ShapeDtypeStruct((1, PTS), F32),
        ),
        in_specs=[vmem] * 5,
        out_specs=(vmem, vmem, vmem),
        scratch_shapes=[
            pltpu.VMEM((NS, 48, DQ), BF16),
            pltpu.VMEM((NS, 48, DQ), BF16),
            pltpu.VMEM((2, NG, 32, D), BF16),
            pltpu.VMEM((NS, 16, DH), BF16),
            pltpu.VMEM((NS, 16, DH), BF16),
            pltpu.VMEM((NS, 1, TILE), I32),
            pltpu.VMEM((NS, 1, TILE), I32),
            pltpu.VMEM((NS, 1, TILE), F32),
            pltpu.VMEM((NS, 1, TILE), F32),
            dma((NS,)), dma((NS,)), dma((NS,)), dma((NS,)),
            dma((2, 2, NZ // 2)), dma((2, NG)), dma((2, 2, NZ // 2 + 1)),
            dma((NS,)), dma((NS,)), dma((NS,)), dma((NS,)),
            pltpu.SemaphoreType.REGULAR((2,)), dma((1,)),
        ],
        compiler_params=pltpu.CompilerParams(
            collective_id=0, has_side_effects=True, vmem_limit_bytes=56 << 20
        ),
        name="fused",
    )(
        points, cen, candidates.T, assign.reshape(1, PTS),
        slot_index.reshape(1, PTS),
    )
    scores, gram, best = pl.pallas_call(
        deliver,
        out_shape=tuple(jax.ShapeDtypeStruct(o.shape, o.dtype) for o in outs),
        in_specs=[vmem] * 3,
        out_specs=(vmem,) * 3,
        compiler_params=pltpu.CompilerParams(vmem_limit_bytes=56 << 20),
        name="deliver",
    )(*outs)
    return scores, gram, best.reshape(PTS)


def solution(mesh):
    in_specs = (
        P(("grp", "shard"), None),
        P("shard", "grp", None),
        P("grp", None),
        P(("grp", "shard")),
        P(("grp", "shard")),
    )
    out_specs = (P(("grp", "shard"), None), P(("grp", "shard"), None, None), P(("grp", "shard")))
    return jax.shard_map(
        on_device, mesh=mesh, in_specs=in_specs, out_specs=out_specs, check_vma=False
    )
```

```python
import functools

import jax
import jax.numpy as jnp
from jax import lax
from jax.experimental import pallas as pl
from jax.experimental.pallas import tpu as pltpu
from jax.sharding import PartitionSpec as P

D = 4096
TILE = 128
K = 2
CAP = 128
PTS = 256
CL = 4
NX, NY, NZ, NC = 4, 8, 12, 2
NS = NX * NY
NG = NZ * NC
TPG = 7
EPS = 1e-06
SCALE = 64.0
Q = 4
DQ = D // Q
DH = D // 2
MESH = pl.DeviceIdType.MESH
HI = lax.Precision.HIGHEST
F32 = jnp.float32
BF16 = jnp.bfloat16
I32 = jnp.int32
NT = (((1,), (1,)), ((), ()))


def iota(shape, dim):
    return lax.broadcasted_iota(I32, shape, dim)


def flag(cond, dtype=F32):
    return jnp.where(cond, 1.0, 0.0).astype(dtype)


def unit(total):
    return lax.rsqrt(total * (1.0 / D) + EPS) * (1.0 / 64.0)


def to_row(column):
    n = column.shape[0]
    return jnp.sum(jnp.where(iota((n, n), 0) == iota((n, n), 1), column, 0), axis=0, keepdims=True)


def zigzag(i, n):
    return lax.rem(jnp.where(lax.rem(i, 2) == 1, (i + 1) // 2, n - i // 2), n)


def kernel(
    pts_hbm, cen, cand, asg, slt,
    out_scores, out_gram, out_best,
    send, got, tiles, csend, cgot, idsend, idgot, repsend, repgot,
    ps, pr, ids_s, ids_r, zs, zr, ks, cs, cr, rs, rr, token, pts, fs,
):
    fetch = pltpu.make_async_copy(pts_hbm, pts, fs.at[0])
    fetch.start()
    grp, me = lax.axis_index("grp"), lax.axis_index("shard")
    z, core = grp // NC, lax.rem(grp, NC)
    x, y = me // NY, lax.rem(me, NY)

    def peer(k):
        xx = lax.rem(x + zigzag(k // NY, NX), NX)
        yy = lax.rem(y + zigzag(lax.rem(k, NY), NY), NY)
        return xx * NY + yy

    up = lax.rem(z + 1, NZ) * NC + core
    down = lax.rem(z + NZ - 1, NZ) * NC + core
    twin = z * NC + (1 - core)
    low, high = z == 0, z == NZ - 1

    barrier = pltpu.get_barrier_semaphore()

    @pl.loop(1, NS)
    def _(k):
        pl.semaphore_signal(barrier, 1, device_id=(grp, peer(k)), device_id_type=MESH)

    pl.semaphore_signal(barrier, 1, device_id=(twin, me), device_id_type=MESH)

    @pl.when(jnp.logical_not(high))
    def _():
        pl.semaphore_signal(barrier, 1, device_id=(up, me), device_id_type=MESH)

    @pl.when(jnp.logical_not(low))
    def _():
        pl.semaphore_signal(barrier, 1, device_id=(down, me), device_id_type=MESH)

    def tile_copy(entry, dest, ssem):
        return pltpu.make_async_remote_copy(
            src_ref=tiles.at[entry], dst_ref=tiles.at[entry], send_sem=ssem,
            recv_sem=zr.at[entry], device_id=(dest, me), device_id_type=MESH,
        )

    owner_row = lax.rem(asg[...] // CL, NS)
    member_row = lax.rem(asg[...], CL) * CAP + slt[...]
    own = flag(iota((NS, PTS), 0) == owner_row)
    before = flag(iota((PTS, PTS), 0) < iota((PTS, PTS), 1), BF16)
    ranks = jnp.dot(own.astype(BF16), before, preferred_element_type=F32)
    rank_row = jnp.sum(own * ranks, axis=0, keepdims=True).astype(I32)
    place_row = owner_row * 16 + rank_row
    at_rank = flag(iota((TILE, PTS), 0) == rank_row)

    def quarter_slot(a, i):
        p = a * 16 + i
        quarter = (p >= 12).astype(I32) + (p >= 24).astype(I32) + (p >= 36).astype(I32)
        return quarter, p - 12 * quarter

    def point_copy(k):
        d = peer(k)
        return pltpu.make_async_remote_copy(
            src_ref=send.at[d], dst_ref=got.at[me], send_sem=ps.at[k], recv_sem=pr.at[me],
            device_id=(grp, d), device_id_type=MESH,
        )

    def id_copy(k):
        d = peer(k)
        return pltpu.make_async_remote_copy(
            src_ref=idsend.at[d], dst_ref=idgot.at[me], send_sem=ids_s.at[k], recv_sem=ids_r.at[me],
            device_id=(grp, d), device_id_type=MESH,
        )

    def build(j):
        xx = lax.rem(x + zigzag(j, NX), NX)
        line = iota((NY * 16, 1), 0)
        for a in range(3):
            quarter, slot = quarter_slot(a, lax.rem(line, 16))
            code = xx * (NY * 16) + line // 16 * 16 + slot
            total = None
            for q in (a, a + 1):
                pick = flag(jnp.where(quarter == q, code, -1) == place_row, BF16)
                part = jnp.dot(pick, pts[:, q * DQ : (q + 1) * DQ], preferred_element_type=F32)
                total = part if total is None else total + part
            send[pl.ds(xx * NY, NY), a * 16 : (a + 1) * 16, :] = total.astype(BF16).reshape(NY, 16, DQ)

    fetch.wait()
    build(0)
    ends = low.astype(I32) + high.astype(I32)
    pl.semaphore_wait(barrier, NS - 1 + 3 - ends)

    @pl.when(low)
    def _():
        pl.semaphore_signal(token.at[0], 1, device_id=(up, me), device_id_type=MESH)

    @pl.when(high)
    def _():
        pl.semaphore_signal(token.at[1], 1, device_id=(down, me), device_id_type=MESH)

    def send_points(j):
        @pl.loop(jnp.where(j == 0, 1, 0), NY)
        def _(i):
            point_copy(j * NY + i).start()

    send_points(0)
    mine = [cen[t].astype(F32) for t in range(TPG)] + [jnp.zeros((4, D), F32)]
    tiles[grp] = jnp.concatenate(mine, axis=0).astype(BF16)

    @pl.when(jnp.logical_not(high))
    def _():
        tile_copy(grp, up, zs.at[0, 0]).start()

    @pl.when(jnp.logical_not(low))
    def _():
        tile_copy(grp, down, zs.at[1, 0]).start()

    tile_copy(grp, twin, ks.at[0, 0]).start()

    @pl.loop(1, NX)
    def _(j):
        build(j)
        send_points(j)

    ids = lax.dot_general(
        own * (member_row + 1).astype(F32), at_rank, NT, precision=HI, preferred_element_type=F32
    )
    ids = (ids + 0.5).astype(I32)
    for o in range(NS):
        idsend[o] = ids[o : o + 1]

    @pl.loop(1, NS)
    def _(k):
        id_copy(k).start()

    got[me] = send[me]
    idgot[me] = idsend[me]

    def token_down():
        pl.semaphore_wait(token.at[1], 1)

        @pl.when(jnp.logical_not(low))
        def _():
            pl.semaphore_signal(token.at[1], 1, device_id=(down, me), device_id_type=MESH)

    @pl.when(jnp.logical_not(low))
    def _():
        pl.semaphore_wait(token.at[0], 1)

        @pl.when(jnp.logical_not(high))
        def _():
            pl.semaphore_signal(token.at[0], 1, device_id=(up, me), device_id_type=MESH)

    @pl.when((z >= NZ // 2) & (z < NZ - 1))
    def _():
        token_down()

    @pl.when(high)
    def _():
        tile_copy(grp, up, zs.at[0, 0]).start()

    reach = (NZ // 2, NZ // 2 - 1)

    def forward(way, step):
        dest, shift = ((up, NZ - step), (down, step))[way]
        entry = lax.rem(z + shift, NZ) * NC + core
        tile_copy(entry, dest, zs.at[way, 0]).wait_recv()

        @pl.when(step < reach[way])
        def _():
            tile_copy(entry, dest, zs.at[way, step]).start()

        tile_copy(entry, twin, ks.at[way, step]).start()

    @pl.loop(1, NZ // 2 + 4)
    def _(t):
        for late in range(2):
            for way in range(2):
                step = t - 3 * late
                if (late, way) == (0, 1):
                    step -= low.astype(I32)
                inside = (z, NZ - 1 - z)[way]
                due = step > inside if late else step <= inside

                @pl.when(due & (step >= 1) & (step <= reach[way]))
                def _():
                    forward(way, step)

        @pl.when((t == 1) & (z < NZ // 2))
        def _():
            token_down()

        @pl.when((t == 1) & low)
        def _():
            tile_copy(grp, down, zs.at[1, 0]).start()

    @pl.loop(0, NZ)
    def _(i):
        tile_copy(i * NC + 1 - core, twin, ks.at[0, 0]).wait_recv()

    line = iota((NS * 8, NS), 0)
    wanted = jnp.zeros((NS * 8, 1), I32)
    for k in range(K):
        here = line // 4 == iota((NS * 8, NS), 1) * K + k
        wanted += jnp.sum(jnp.where(here, cand[k : k + 1], 0), axis=1, keepdims=True)
    first = (wanted * 9363) >> 16
    code = first * 32 + (wanted - first * TPG) * 4 + lax.rem(iota((NS * 8, 1), 0), 4)
    pick = flag(code == iota((NS * 8, NG * 32), 1), BF16)

    @pl.loop(0, DH // 512)
    def _(i):
        halves = []
        for h in range(2):
            cols = pl.ds(pl.multiple_of(h * DH + i * 512, 512), 512)
            block = tiles[:, :, cols].reshape(NG * 32, 512)
            halves.append(jnp.dot(pick, block, preferred_element_type=F32).reshape(NS, 8, 512))
        both = jnp.concatenate(halves, axis=1).astype(BF16)
        csend[:, :, pl.ds(pl.multiple_of(i * 512, 512), 512)] = both

    def cen_copy(k):
        d = peer(k)
        return pltpu.make_async_remote_copy(
            src_ref=csend.at[d], dst_ref=cgot.at[me], send_sem=cs.at[k], recv_sem=cr.at[me],
            device_id=(grp, d), device_id_type=MESH,
        )

    @pl.loop(1, NS)
    def _(k):
        cen_copy(k).start()

    cgot[me] = csend[me]

    wide = pts[...].astype(F32)
    point_unit = unit(jnp.sum(wide * wide, axis=1, keepdims=True))

    def arrive(dst, sem, d):
        pltpu.make_async_remote_copy(
            src_ref=dst.at[d], dst_ref=dst.at[d], send_sem=ps.at[0], recv_sem=sem.at[d],
            device_id=(grp, d), device_id_type=MESH,
        ).wait_recv()

    @pl.loop(1, NS)
    def _(k):
        arrive(idgot, ids_r, peer(k))
        arrive(got, pr, peer(k))

    idm = jnp.concatenate([idgot[o] for o in range(NS)], axis=0).astype(F32)
    lane = iota((1, NS * 16), 1)
    mine = iota((NS, NS * 16), 0) == iota((NS, NS * 16), 1) // 16

    def scatter(q, a):
        quarter, slot = quarter_slot(a, lax.rem(lane, 16))
        slot = jnp.where(quarter == q, slot, -1)
        spread = flag(iota((TILE, NS * 16), 0) == slot)
        ids = jnp.dot(idm, spread, precision=HI, preferred_element_type=F32)
        row = jnp.sum(jnp.where(mine, ids, 0.0), axis=0, keepdims=True)
        row = (row + 0.5).astype(I32)
        return iota((CL * CAP, NS * 16), 0) + 1 == row

    full = flag(scatter(0, 0))
    grams = [jnp.zeros((CAP, CAP), F32) for _ in range(CL)]
    for q in range(Q):
        maps = [(a, flag(scatter(q, a), BF16)) for a in (q - 1, q) if 0 <= a < 3]

        def step(i, acc):
            cols = pl.ds(pl.multiple_of(i * 256, 256), 256)
            rows = None
            for a, m in maps:
                block = got[:, a * 16 : (a + 1) * 16, cols].reshape(NS * 16, 256)
                part = jnp.dot(m, block, preferred_element_type=F32)
                rows = part if rows is None else rows + part
            rows = rows.astype(BF16)
            out = []
            for c in range(CL):
                r = rows[c * CAP : (c + 1) * CAP]
                out.append(acc[c] + lax.dot_general(r, r, NT, preferred_element_type=F32))
            return out

        grams = lax.fori_loop(0, DQ // 256, step, grams)

    occupied = jnp.sum(full, axis=1, keepdims=True)
    diagonal = iota((CAP, CAP), 0) == iota((CAP, CAP), 1)
    bests = []
    for c in range(CL):
        g = grams[c]
        d = jnp.where(diagonal, g, 0.0)
        u_col = unit(jnp.sum(d, axis=1, keepdims=True))
        u_row = unit(jnp.sum(d, axis=0, keepdims=True))
        g = SCALE * g * u_col * u_row
        out_gram[c] = g
        others = flag((occupied[c * CAP : (c + 1) * CAP] > 0.5) & jnp.logical_not(diagonal))
        best = jnp.max(jnp.where(others > 0.5, g, -jnp.inf), axis=0, keepdims=True)
        some = jnp.max(others, axis=0, keepdims=True) > 0.5
        bests.append(jnp.where(some, best, 0.0))
    best = jnp.concatenate(bests, axis=1)

    rep = jnp.dot(
        jnp.broadcast_to(best, (8, CL * CAP)), full, precision=HI, preferred_element_type=F32
    )[0:1]
    slots = flag(lax.rem(iota((NS * 16, TILE), 0), 16) == iota((NS * 16, TILE), 1))
    rep = jnp.dot(jnp.where(mine, rep, 0.0), slots, precision=HI, preferred_element_type=F32)
    for o in range(NS):
        repsend[o] = rep[o : o + 1]

    def rep_copy(k):
        d = peer(k)
        return pltpu.make_async_remote_copy(
            src_ref=repsend.at[d], dst_ref=repgot.at[me], send_sem=rs.at[k], recv_sem=rr.at[me],
            device_id=(grp, d), device_id_type=MESH,
        )

    @pl.loop(1, NS)
    def _(k):
        rep_copy(k).start()

    repgot[me] = repsend[me]

    @pl.loop(1, NS)
    def _(k):
        point_copy(k).wait_send()
        id_copy(k).wait_send()

    tile_copy(grp, twin, ks.at[0, 0]).wait_send()
    for way in range(2):
        for step in range(reach[way]):
            tile_copy(grp, up, zs.at[way, step]).wait_send()
            tile_copy(grp, twin, ks.at[way, step + 1]).wait_send()

    out_scores[...] = jnp.zeros((PTS, K * TILE), F32)
    line = iota((NY * 8, 1), 0)
    base = lax.rem(line, NY * 4) // 4 * 16 + line // (NY * 4) * 4 + lax.rem(line, 4)
    column = line // (NY * 4) * TILE + lax.rem(line, NY * 4)

    def column_scores(j):
        xx = lax.rem(x - zigzag(j, NX) + NX, NX)

        @pl.loop(jnp.where(j == 0, 1, 0), NY)
        def _(i):
            arrive(cgot, cr, xx * NY + lax.rem(y - zigzag(i, NY) + NY, NY))

        def score(i, acc):
            dots, squares = acc
            for h in range(2):
                perm = flag(base + h * 8 == iota((NY * 8, NY * 16), 1), BF16)
                cols = pl.ds(pl.multiple_of(i * 512, 512), 512)
                block = cgot[pl.ds(xx * NY, NY), :, cols].reshape(NY * 16, 512)
                rows = jnp.dot(perm, block, preferred_element_type=F32)
                squares = squares + jnp.sum(rows * rows, axis=1, keepdims=True)
                p = pts[:, pl.ds(pl.multiple_of(h * DH + i * 512, 512), 512)]
                dots = dots + lax.dot_general(p, rows.astype(BF16), NT, preferred_element_type=F32)
            return dots, squares

        dots, squares = lax.fori_loop(
            0, DH // 512, score, (jnp.zeros((PTS, NY * 8), F32), jnp.zeros((NY * 8, 1), F32))
        )
        put = flag(column + xx * (NY * 4) == iota((NY * 8, K * TILE), 1))
        dots = SCALE * dots * point_unit * to_row(unit(squares))
        out_scores[...] += jnp.dot(dots, put, precision=HI, preferred_element_type=F32)

        @pl.loop(jnp.where(j == 0, 1, 0), NY)
        def _(i):
            cen_copy(j * NY + i).wait_send()

    @pl.loop(0, NX - 1)
    def _(j):
        column_scores(j)

    @pl.loop(1, NS)
    def _(k):
        arrive(repgot, rr, peer(k))

    rep = jnp.concatenate([repgot[o] for o in range(NS)], axis=0)
    back = jnp.dot(rep, at_rank, precision=HI, preferred_element_type=F32)
    out_best[...] = jnp.sum(own * back, axis=0, keepdims=True)

    @pl.loop(1, NS)
    def _(k):
        rep_copy(k).wait_send()

    column_scores(NX - 1)


def deliver(a, b, c, out_a, out_b, out_c):
    out_a[...] = a[...]
    out_b[...] = b[...]
    out_c[...] = c[...]


def on_device(points, centroids, candidates, assign, slot_index):
    cen = jnp.transpose(centroids, (1, 0, 2))
    dma = pltpu.SemaphoreType.DMA
    vmem = pl.BlockSpec(memory_space=pltpu.VMEM)
    outs = pl.pallas_call(
        kernel,
        out_shape=(
            jax.ShapeDtypeStruct((PTS, K * TILE), F32),
            jax.ShapeDtypeStruct((CL, CAP, CAP), F32),
            jax.ShapeDtypeStruct((1, PTS), F32),
        ),
        in_specs=[pl.BlockSpec(memory_space=pl.ANY)] + [vmem] * 4,
        out_specs=(vmem, vmem, vmem),
        scratch_shapes=[
            pltpu.VMEM((NS, 48, DQ), BF16),
            pltpu.VMEM((NS, 48, DQ), BF16),
            pltpu.VMEM((NG, 32, D), BF16),
            pltpu.VMEM((NS, 16, DH), BF16),
            pltpu.VMEM((NS, 16, DH), BF16),
            pltpu.VMEM((NS, 1, TILE), I32),
            pltpu.VMEM((NS, 1, TILE), I32),
            pltpu.VMEM((NS, 1, TILE), F32),
            pltpu.VMEM((NS, 1, TILE), F32),
            dma((NS,)), dma((NS,)), dma((NS,)), dma((NS,)),
            dma((2, NZ // 2)), dma((NG,)), dma((2, NZ // 2 + 1)),
            dma((NS,)), dma((NS,)), dma((NS,)), dma((NS,)),
            pltpu.SemaphoreType.REGULAR((2,)),
            pltpu.VMEM((PTS, D), BF16), dma((1,)),
        ],
        compiler_params=pltpu.CompilerParams(
            collective_id=0, has_side_effects=True, vmem_limit_bytes=56 << 20
        ),
        name="fused",
    )(
        points, cen, candidates.T, assign.reshape(1, PTS),
        slot_index.reshape(1, PTS),
    )
    scores, gram, best = pl.pallas_call(
        deliver,
        out_shape=tuple(jax.ShapeDtypeStruct(o.shape, o.dtype) for o in outs),
        in_specs=[vmem] * 3,
        out_specs=(vmem,) * 3,
        compiler_params=pltpu.CompilerParams(vmem_limit_bytes=56 << 20),
        name="deliver",
    )(*outs)
    return scores, gram, best.reshape(PTS)


def solution(mesh):
    in_specs = (
        P(("grp", "shard"), None),
        P("shard", "grp", None),
        P("grp", None),
        P(("grp", "shard")),
        P(("grp", "shard")),
    )
    out_specs = (P(("grp", "shard"), None), P(("grp", "shard"), None, None), P(("grp", "shard")))
    return jax.shard_map(
        on_device, mesh=mesh, in_specs=in_specs, out_specs=out_specs, check_vma=False
    )
```

```python
import functools

import jax
import jax.numpy as jnp
from jax import lax
from jax.experimental import pallas as pl
from jax.experimental.pallas import tpu as pltpu
from jax.sharding import PartitionSpec as P

D = 4096
TILE = 128
K = 2
CAP = 128
PTS = 256
CL = 4
NX, NY, NZ, NC = 4, 8, 12, 2
NS = NX * NY
NG = NZ * NC
TPG = 7
EPS = 1e-06
SCALE = 64.0
Q = 4
DQ = D // Q
DH = D // 2
MESH = pl.DeviceIdType.MESH
HI = lax.Precision.HIGHEST
F32 = jnp.float32
BF16 = jnp.bfloat16
I32 = jnp.int32
NT = (((1,), (1,)), ((), ()))


def iota(shape, dim):
    return lax.broadcasted_iota(I32, shape, dim)


def flag(cond, dtype=F32):
    return jnp.where(cond, 1.0, 0.0).astype(dtype)


def unit(total):
    return lax.rsqrt(total * (1.0 / D) + EPS) * (1.0 / 64.0)


def to_row(column):
    n = column.shape[0]
    return jnp.sum(jnp.where(iota((n, n), 0) == iota((n, n), 1), column, 0), axis=0, keepdims=True)


def zigzag(i, n):
    return lax.rem(jnp.where(lax.rem(i, 2) == 1, (i + 1) // 2, n - i // 2), n)


def kernel(
    pts_hbm, cen, cand, asg, slt,
    out_scores, out_gram, out_best,
    send, got, tiles, csend, cgot, idsend, idgot, repsend, repgot,
    ps, pr, ids_s, ids_r, zs, zr, ks, cs, cr, rs, rr, token, pts, fs,
):
    fetch = pltpu.make_async_copy(pts_hbm, pts, fs.at[0])
    fetch.start()
    grp, me = lax.axis_index("grp"), lax.axis_index("shard")
    z, core = grp // NC, lax.rem(grp, NC)
    x, y = me // NY, lax.rem(me, NY)

    def peer(k):
        xx = lax.rem(x + zigzag(k // NY, NX), NX)
        yy = lax.rem(y + zigzag(lax.rem(k, NY), NY), NY)
        return xx * NY + yy

    up = lax.rem(z + 1, NZ) * NC + core
    down = lax.rem(z + NZ - 1, NZ) * NC + core
    twin = z * NC + (1 - core)
    low, high = z == 0, z == NZ - 1

    barrier = pltpu.get_barrier_semaphore()

    @pl.loop(1, NS)
    def _(k):
        pl.semaphore_signal(barrier, 1, device_id=(grp, peer(k)), device_id_type=MESH)

    pl.semaphore_signal(barrier, 1, device_id=(twin, me), device_id_type=MESH)

    @pl.when(jnp.logical_not(high))
    def _():
        pl.semaphore_signal(barrier, 1, device_id=(up, me), device_id_type=MESH)

    @pl.when(jnp.logical_not(low))
    def _():
        pl.semaphore_signal(barrier, 1, device_id=(down, me), device_id_type=MESH)

    def tile_copy(entry, dest, ssem):
        return pltpu.make_async_remote_copy(
            src_ref=tiles.at[entry], dst_ref=tiles.at[entry], send_sem=ssem,
            recv_sem=zr.at[entry], device_id=(dest, me), device_id_type=MESH,
        )

    owner_row = lax.rem(asg[...] // CL, NS)
    member_row = lax.rem(asg[...], CL) * CAP + slt[...]
    own = flag(iota((NS, PTS), 0) == owner_row)
    before = flag(iota((PTS, PTS), 0) < iota((PTS, PTS), 1), BF16)
    ranks = jnp.dot(own.astype(BF16), before, preferred_element_type=F32)
    rank_row = jnp.sum(own * ranks, axis=0, keepdims=True).astype(I32)
    place_row = owner_row * 16 + rank_row
    at_rank = flag(iota((TILE, PTS), 0) == rank_row)

    def quarter_slot(a, i):
        p = a * 16 + i
        quarter = (p >= 12).astype(I32) + (p >= 24).astype(I32) + (p >= 36).astype(I32)
        return quarter, p - 12 * quarter

    def point_copy(k):
        d = peer(k)
        return pltpu.make_async_remote_copy(
            src_ref=send.at[d], dst_ref=got.at[me], send_sem=ps.at[k], recv_sem=pr.at[me],
            device_id=(grp, d), device_id_type=MESH,
        )

    def id_copy(k):
        d = peer(k)
        return pltpu.make_async_remote_copy(
            src_ref=idsend.at[d], dst_ref=idgot.at[me], send_sem=ids_s.at[k], recv_sem=ids_r.at[me],
            device_id=(grp, d), device_id_type=MESH,
        )

    def build(j):
        xx = lax.rem(x + zigzag(j, NX), NX)
        line = iota((NY * 16, 1), 0)
        for a in range(3):
            quarter, slot = quarter_slot(a, lax.rem(line, 16))
            code = xx * (NY * 16) + line // 16 * 16 + slot
            total = None
            for q in (a, a + 1):
                pick = flag(jnp.where(quarter == q, code, -1) == place_row, BF16)
                part = jnp.dot(pick, pts[:, q * DQ : (q + 1) * DQ], preferred_element_type=F32)
                total = part if total is None else total + part
            send[pl.ds(xx * NY, NY), a * 16 : (a + 1) * 16, :] = total.astype(BF16).reshape(NY, 16, DQ)

    fetch.wait()
    build(0)
    ends = low.astype(I32) + high.astype(I32)
    pl.semaphore_wait(barrier, NS - 1 + 3 - ends)

    @pl.when(low)
    def _():
        pl.semaphore_signal(token.at[0], 1, device_id=(up, me), device_id_type=MESH)

    @pl.when(high)
    def _():
        pl.semaphore_signal(token.at[1], 1, device_id=(down, me), device_id_type=MESH)

    def send_points(j):
        @pl.loop(jnp.where(j == 0, 1, 0), NY)
        def _(i):
            point_copy(j * NY + i).start()

    send_points(0)

    def token_down():
        pl.semaphore_wait(token.at[1], 1)

        @pl.when(jnp.logical_not(low))
        def _():
            pl.semaphore_signal(token.at[1], 1, device_id=(down, me), device_id_type=MESH)

    @pl.when(jnp.logical_not(low))
    def _():
        pl.semaphore_wait(token.at[0], 1)

        @pl.when(jnp.logical_not(high))
        def _():
            pl.semaphore_signal(token.at[0], 1, device_id=(up, me), device_id_type=MESH)

    @pl.when((z >= NZ // 2) & (z < NZ - 1))
    def _():
        token_down()

    mine = [cen[t].astype(F32) for t in range(TPG)] + [jnp.zeros((4, D), F32)]
    tiles[grp] = jnp.concatenate(mine, axis=0).astype(BF16)

    tile_copy(grp, up, zs.at[0, 0]).start()

    @pl.when(jnp.logical_not(low))
    def _():
        tile_copy(grp, down, zs.at[1, 0]).start()

    tile_copy(grp, twin, ks.at[0, 0]).start()

    @pl.loop(1, NX)
    def _(j):
        build(j)
        send_points(j)

    ids = lax.dot_general(
        own * (member_row + 1).astype(F32), at_rank, NT, precision=HI, preferred_element_type=F32
    )
    ids = (ids + 0.5).astype(I32)
    for o in range(NS):
        idsend[o] = ids[o : o + 1]

    @pl.loop(1, NS)
    def _(k):
        id_copy(k).start()

    got[me] = send[me]
    idgot[me] = idsend[me]

    @pl.when((z >= NZ // 4) & (z < NZ // 2))
    def _():
        token_down()

    reach = (NZ // 2, NZ // 2 - 1)

    def forward(way, step):
        dest, shift = ((up, NZ - step), (down, step))[way]
        entry = lax.rem(z + shift, NZ) * NC + core
        tile_copy(entry, dest, zs.at[way, 0]).wait_recv()

        @pl.when(step < reach[way])
        def _():
            tile_copy(entry, dest, zs.at[way, step]).start()

        tile_copy(entry, twin, ks.at[way, step]).start()

    @pl.loop(1, NZ // 2 + 2)
    def _(t):
        for late in range(2):
            for way in range(2):
                step = t - late
                if (late, way) == (0, 1):
                    step -= low.astype(I32)
                inside = (z, NZ - 1 - z)[way]
                due = step > inside if late else step <= inside

                @pl.when(due & (step >= 1) & (step <= reach[way]))
                def _():
                    forward(way, step)

        @pl.when((t == 1) & (z < NZ // 4))
        def _():
            token_down()

        @pl.when((t == 1) & low)
        def _():
            tile_copy(grp, down, zs.at[1, 0]).start()

    @pl.loop(0, NZ)
    def _(i):
        tile_copy(i * NC + 1 - core, twin, ks.at[0, 0]).wait_recv()

    line = iota((NS * 8, NS), 0)
    wanted = jnp.zeros((NS * 8, 1), I32)
    for k in range(K):
        here = line // 4 == iota((NS * 8, NS), 1) * K + k
        wanted += jnp.sum(jnp.where(here, cand[k : k + 1], 0), axis=1, keepdims=True)
    first = (wanted * 9363) >> 16
    code = first * 32 + (wanted - first * TPG) * 4 + lax.rem(iota((NS * 8, 1), 0), 4)
    pick = flag(code == iota((NS * 8, NG * 32), 1), BF16)

    @pl.loop(0, DH // 512)
    def _(i):
        halves = []
        for h in range(2):
            cols = pl.ds(pl.multiple_of(h * DH + i * 512, 512), 512)
            block = tiles[:, :, cols].reshape(NG * 32, 512)
            halves.append(jnp.dot(pick, block, preferred_element_type=F32).reshape(NS, 8, 512))
        both = jnp.concatenate(halves, axis=1).astype(BF16)
        csend[:, :, pl.ds(pl.multiple_of(i * 512, 512), 512)] = both

    def cen_copy(k):
        d = peer(k)
        return pltpu.make_async_remote_copy(
            src_ref=csend.at[d], dst_ref=cgot.at[me], send_sem=cs.at[k], recv_sem=cr.at[me],
            device_id=(grp, d), device_id_type=MESH,
        )

    @pl.loop(1, NS)
    def _(k):
        cen_copy(k).start()

    cgot[me] = csend[me]

    wide = pts[...].astype(F32)
    point_unit = unit(jnp.sum(wide * wide, axis=1, keepdims=True))

    def arrive(dst, sem, d):
        pltpu.make_async_remote_copy(
            src_ref=dst.at[d], dst_ref=dst.at[d], send_sem=ps.at[0], recv_sem=sem.at[d],
            device_id=(grp, d), device_id_type=MESH,
        ).wait_recv()

    @pl.loop(1, NS)
    def _(k):
        arrive(idgot, ids_r, peer(k))
        arrive(got, pr, peer(k))

    idm = jnp.concatenate([idgot[o] for o in range(NS)], axis=0).astype(F32)
    lane = iota((1, NS * 16), 1)
    mine = iota((NS, NS * 16), 0) == iota((NS, NS * 16), 1) // 16

    def scatter(q, a):
        quarter, slot = quarter_slot(a, lax.rem(lane, 16))
        slot = jnp.where(quarter == q, slot, -1)
        spread = flag(iota((TILE, NS * 16), 0) == slot)
        ids = jnp.dot(idm, spread, precision=HI, preferred_element_type=F32)
        row = jnp.sum(jnp.where(mine, ids, 0.0), axis=0, keepdims=True)
        row = (row + 0.5).astype(I32)
        return iota((CL * CAP, NS * 16), 0) + 1 == row

    full = flag(scatter(0, 0))
    grams = [jnp.zeros((CAP, CAP), F32) for _ in range(CL)]
    for q in range(Q):
        maps = [(a, flag(scatter(q, a), BF16)) for a in (q - 1, q) if 0 <= a < 3]

        def step(i, acc):
            cols = pl.ds(pl.multiple_of(i * 256, 256), 256)
            rows = None
            for a, m in maps:
                block = got[:, a * 16 : (a + 1) * 16, cols].reshape(NS * 16, 256)
                part = jnp.dot(m, block, preferred_element_type=F32)
                rows = part if rows is None else rows + part
            rows = rows.astype(BF16)
            out = []
            for c in range(CL):
                r = rows[c * CAP : (c + 1) * CAP]
                out.append(acc[c] + lax.dot_general(r, r, NT, preferred_element_type=F32))
            return out

        grams = lax.fori_loop(0, DQ // 256, step, grams)

    occupied = jnp.sum(full, axis=1, keepdims=True)
    diagonal = iota((CAP, CAP), 0) == iota((CAP, CAP), 1)
    bests = []
    for c in range(CL):
        g = grams[c]
        d = jnp.where(diagonal, g, 0.0)
        u_col = unit(jnp.sum(d, axis=1, keepdims=True))
        u_row = unit(jnp.sum(d, axis=0, keepdims=True))
        g = SCALE * g * u_col * u_row
        out_gram[c] = g
        others = flag((occupied[c * CAP : (c + 1) * CAP] > 0.5) & jnp.logical_not(diagonal))
        best = jnp.max(jnp.where(others > 0.5, g, -jnp.inf), axis=0, keepdims=True)
        some = jnp.max(others, axis=0, keepdims=True) > 0.5
        bests.append(jnp.where(some, best, 0.0))
    best = jnp.concatenate(bests, axis=1)

    rep = jnp.dot(
        jnp.broadcast_to(best, (8, CL * CAP)), full, precision=HI, preferred_element_type=F32
    )[0:1]
    slots = flag(lax.rem(iota((NS * 16, TILE), 0), 16) == iota((NS * 16, TILE), 1))
    rep = jnp.dot(jnp.where(mine, rep, 0.0), slots, precision=HI, preferred_element_type=F32)
    for o in range(NS):
        repsend[o] = rep[o : o + 1]

    def rep_copy(k):
        d = peer(k)
        return pltpu.make_async_remote_copy(
            src_ref=repsend.at[d], dst_ref=repgot.at[me], send_sem=rs.at[k], recv_sem=rr.at[me],
            device_id=(grp, d), device_id_type=MESH,
        )

    @pl.loop(1, NS)
    def _(k):
        rep_copy(k).start()

    repgot[me] = repsend[me]

    @pl.loop(1, NS)
    def _(k):
        point_copy(k).wait_send()
        id_copy(k).wait_send()

    tile_copy(grp, twin, ks.at[0, 0]).wait_send()
    for way in range(2):
        for step in range(reach[way]):
            tile_copy(grp, up, zs.at[way, step]).wait_send()
            tile_copy(grp, twin, ks.at[way, step + 1]).wait_send()

    out_scores[...] = jnp.zeros((PTS, K * TILE), F32)
    line = iota((NY * 8, 1), 0)
    base = lax.rem(line, NY * 4) // 4 * 16 + line // (NY * 4) * 4 + lax.rem(line, 4)
    column = line // (NY * 4) * TILE + lax.rem(line, NY * 4)

    def column_scores(j):
        xx = lax.rem(x - zigzag(j, NX) + NX, NX)

        @pl.loop(jnp.where(j == 0, 1, 0), NY)
        def _(i):
            arrive(cgot, cr, xx * NY + lax.rem(y - zigzag(i, NY) + NY, NY))

        def score(i, acc):
            dots, squares = acc
            for h in range(2):
                perm = flag(base + h * 8 == iota((NY * 8, NY * 16), 1), BF16)
                cols = pl.ds(pl.multiple_of(i * 512, 512), 512)
                block = cgot[pl.ds(xx * NY, NY), :, cols].reshape(NY * 16, 512)
                rows = jnp.dot(perm, block, preferred_element_type=F32)
                squares = squares + jnp.sum(rows * rows, axis=1, keepdims=True)
                p = pts[:, pl.ds(pl.multiple_of(h * DH + i * 512, 512), 512)]
                dots = dots + lax.dot_general(p, rows.astype(BF16), NT, preferred_element_type=F32)
            return dots, squares

        dots, squares = lax.fori_loop(
            0, DH // 512, score, (jnp.zeros((PTS, NY * 8), F32), jnp.zeros((NY * 8, 1), F32))
        )
        put = flag(column + xx * (NY * 4) == iota((NY * 8, K * TILE), 1))
        dots = SCALE * dots * point_unit * to_row(unit(squares))
        out_scores[...] += jnp.dot(dots, put, precision=HI, preferred_element_type=F32)

        @pl.loop(jnp.where(j == 0, 1, 0), NY)
        def _(i):
            cen_copy(j * NY + i).wait_send()

    @pl.loop(0, NX - 1)
    def _(j):
        column_scores(j)

    @pl.loop(1, NS)
    def _(k):
        arrive(repgot, rr, peer(k))

    rep = jnp.concatenate([repgot[o] for o in range(NS)], axis=0)
    back = jnp.dot(rep, at_rank, precision=HI, preferred_element_type=F32)
    out_best[...] = jnp.sum(own * back, axis=0, keepdims=True)

    @pl.loop(1, NS)
    def _(k):
        rep_copy(k).wait_send()

    column_scores(NX - 1)


def deliver(a, b, c, out_a, out_b, out_c):
    out_a[...] = a[...]
    out_b[...] = b[...]
    out_c[...] = c[...]


def on_device(points, centroids, candidates, assign, slot_index):
    cen = jnp.transpose(centroids, (1, 0, 2))
    dma = pltpu.SemaphoreType.DMA
    vmem = pl.BlockSpec(memory_space=pltpu.VMEM)
    outs = pl.pallas_call(
        kernel,
        out_shape=(
            jax.ShapeDtypeStruct((PTS, K * TILE), F32),
            jax.ShapeDtypeStruct((CL, CAP, CAP), F32),
            jax.ShapeDtypeStruct((1, PTS), F32),
        ),
        in_specs=[pl.BlockSpec(memory_space=pl.ANY)] + [vmem] * 4,
        out_specs=(vmem, vmem, vmem),
        scratch_shapes=[
            pltpu.VMEM((NS, 48, DQ), BF16),
            pltpu.VMEM((NS, 48, DQ), BF16),
            pltpu.VMEM((NG, 32, D), BF16),
            pltpu.VMEM((NS, 16, DH), BF16),
            pltpu.VMEM((NS, 16, DH), BF16),
            pltpu.VMEM((NS, 1, TILE), I32),
            pltpu.VMEM((NS, 1, TILE), I32),
            pltpu.VMEM((NS, 1, TILE), F32),
            pltpu.VMEM((NS, 1, TILE), F32),
            dma((NS,)), dma((NS,)), dma((NS,)), dma((NS,)),
            dma((2, NZ // 2)), dma((NG,)), dma((2, NZ // 2 + 1)),
            dma((NS,)), dma((NS,)), dma((NS,)), dma((NS,)),
            pltpu.SemaphoreType.REGULAR((2,)),
            pltpu.VMEM((PTS, D), BF16), dma((1,)),
        ],
        compiler_params=pltpu.CompilerParams(
            collective_id=0, has_side_effects=True, vmem_limit_bytes=56 << 20
        ),
        name="fused",
    )(
        points, cen, candidates.T, assign.reshape(1, PTS),
        slot_index.reshape(1, PTS),
    )
    scores, gram, best = pl.pallas_call(
        deliver,
        out_shape=tuple(jax.ShapeDtypeStruct(o.shape, o.dtype) for o in outs),
        in_specs=[vmem] * 3,
        out_specs=(vmem,) * 3,
        compiler_params=pltpu.CompilerParams(vmem_limit_bytes=56 << 20),
        name="deliver",
    )(*outs)
    return scores, gram, best.reshape(PTS)


def solution(mesh):
    in_specs = (
        P(("grp", "shard"), None),
        P("shard", "grp", None),
        P("grp", None),
        P(("grp", "shard")),
        P(("grp", "shard")),
    )
    out_specs = (P(("grp", "shard"), None), P(("grp", "shard"), None, None), P(("grp", "shard")))
    return jax.shard_map(
        on_device, mesh=mesh, in_specs=in_specs, out_specs=out_specs, check_vma=False
    )
```

```python
import functools

import jax
import jax.numpy as jnp
from jax import lax
from jax.experimental import pallas as pl
from jax.experimental.pallas import tpu as pltpu
from jax.sharding import PartitionSpec as P

D = 4096
TILE = 128
K = 2
CAP = 128
PTS = 256
CL = 4
NX, NY, NZ, NC = 4, 8, 12, 2
NS = NX * NY
NG = NZ * NC
TPG = 7
EPS = 1e-06
SCALE = 64.0
Q = 4
DQ = D // Q
DH = D // 2
MESH = pl.DeviceIdType.MESH
HI = lax.Precision.HIGHEST
F32 = jnp.float32
BF16 = jnp.bfloat16
I32 = jnp.int32
NT = (((1,), (1,)), ((), ()))


def iota(shape, dim):
    return lax.broadcasted_iota(I32, shape, dim)


def flag(cond, dtype=F32):
    return jnp.where(cond, 1.0, 0.0).astype(dtype)


def unit(total):
    return lax.rsqrt(total * (1.0 / D) + EPS) * (1.0 / 64.0)


def to_row(column):
    n = column.shape[0]
    return jnp.sum(jnp.where(iota((n, n), 0) == iota((n, n), 1), column, 0), axis=0, keepdims=True)


def zigzag(i, n):
    return lax.rem(jnp.where(lax.rem(i, 2) == 1, (i + 1) // 2, n - i // 2), n)


def kernel(
    pts_hbm, cen, cand, asg, slt,
    out_scores, out_gram, out_best,
    send, got, tiles, csend, cgot, idsend, idgot, repsend, repgot,
    ps, pr, ids_s, ids_r, zs, zr, ks, cs, cr, rs, rr, token, here, pts, fs,
):
    fetch = pltpu.make_async_copy(pts_hbm, pts, fs.at[0])
    fetch.start()
    grp, me = lax.axis_index("grp"), lax.axis_index("shard")
    z, core = grp // NC, lax.rem(grp, NC)
    x, y = me // NY, lax.rem(me, NY)

    def peer(k):
        xx = lax.rem(x + zigzag(k // NY, NX), NX)
        yy = lax.rem(y + zigzag(lax.rem(k, NY), NY), NY)
        return xx * NY + yy

    up = lax.rem(z + 1, NZ) * NC + core
    down = lax.rem(z + NZ - 1, NZ) * NC + core
    twin = z * NC + (1 - core)
    low, high = z == 0, z == NZ - 1

    last = (grp == 0) & (me == 0)
    beside = (grp == 0) & (me != 0)
    over = (grp == 1) & (me == 0)
    above = (grp == NC) & (me == 0)
    barrier = pltpu.get_barrier_semaphore()

    @pl.when(jnp.logical_not(last))
    def _():
        @pl.loop(1, NS)
        def _(k):
            pl.semaphore_signal(barrier, 1, device_id=(grp, peer(k)), device_id_type=MESH)

        pl.semaphore_signal(barrier, 1, device_id=(twin, me), device_id_type=MESH)

        @pl.when(jnp.logical_not(high))
        def _():
            pl.semaphore_signal(barrier, 1, device_id=(up, me), device_id_type=MESH)

        @pl.when(jnp.logical_not(low))
        def _():
            pl.semaphore_signal(barrier, 1, device_id=(down, me), device_id_type=MESH)

    def tile_copy(entry, dest, ssem):
        return pltpu.make_async_remote_copy(
            src_ref=tiles.at[entry], dst_ref=tiles.at[entry], send_sem=ssem,
            recv_sem=zr.at[entry], device_id=(dest, me), device_id_type=MESH,
        )

    owner_row = lax.rem(asg[...] // CL, NS)
    member_row = lax.rem(asg[...], CL) * CAP + slt[...]
    own = flag(iota((NS, PTS), 0) == owner_row)
    before = flag(iota((PTS, PTS), 0) < iota((PTS, PTS), 1), BF16)
    ranks = jnp.dot(own.astype(BF16), before, preferred_element_type=F32)
    rank_row = jnp.sum(own * ranks, axis=0, keepdims=True).astype(I32)
    place_row = owner_row * 16 + rank_row
    at_rank = flag(iota((TILE, PTS), 0) == rank_row)

    def quarter_slot(a, i):
        p = a * 16 + i
        quarter = (p >= 12).astype(I32) + (p >= 24).astype(I32) + (p >= 36).astype(I32)
        return quarter, p - 12 * quarter

    def point_copy(k):
        d = peer(k)
        return pltpu.make_async_remote_copy(
            src_ref=send.at[d], dst_ref=got.at[me], send_sem=ps.at[k], recv_sem=pr.at[me],
            device_id=(grp, d), device_id_type=MESH,
        )

    def id_copy(k):
        d = peer(k)
        return pltpu.make_async_remote_copy(
            src_ref=idsend.at[d], dst_ref=idgot.at[me], send_sem=ids_s.at[k], recv_sem=ids_r.at[me],
            device_id=(grp, d), device_id_type=MESH,
        )

    def build(j):
        xx = lax.rem(x + zigzag(j, NX), NX)
        line = iota((NY * 16, 1), 0)
        for a in range(3):
            quarter, slot = quarter_slot(a, lax.rem(line, 16))
            code = xx * (NY * 16) + line // 16 * 16 + slot
            total = None
            for q in (a, a + 1):
                pick = flag(jnp.where(quarter == q, code, -1) == place_row, BF16)
                part = jnp.dot(pick, pts[:, q * DQ : (q + 1) * DQ], preferred_element_type=F32)
                total = part if total is None else total + part
            send[pl.ds(xx * NY, NY), a * 16 : (a + 1) * 16, :] = total.astype(BF16).reshape(NY, 16, DQ)

    fetch.wait()
    build(0)
    fewer = (low | high).astype(I32) + (beside | over | above).astype(I32)
    pl.semaphore_wait(barrier, NS - 1 + 3 - fewer)

    @pl.when(last)
    def _():
        @pl.loop(1, NS)
        def _(k):
            pl.semaphore_signal(here, 1, device_id=(grp, peer(k)), device_id_type=MESH)

        pl.semaphore_signal(here, 1, device_id=(twin, me), device_id_type=MESH)

    @pl.when(low)
    def _():
        pl.semaphore_signal(token.at[0], 1, device_id=(up, me), device_id_type=MESH)

    @pl.when(high)
    def _():
        pl.semaphore_signal(token.at[1], 1, device_id=(down, me), device_id_type=MESH)

    def send_points(j):
        @pl.loop(jnp.where(j == 0, 1, 0), NY)
        def _(i):
            @pl.when(jnp.logical_not(beside & (peer(j * NY + i) == 0)))
            def _():
                point_copy(j * NY + i).start()

    send_points(0)

    def token_down():
        pl.semaphore_wait(token.at[1], 1)

        @pl.when(jnp.logical_not(low))
        def _():
            pl.semaphore_signal(token.at[1], 1, device_id=(down, me), device_id_type=MESH)

    @pl.when(jnp.logical_not(low))
    def _():
        pl.semaphore_wait(token.at[0], 1)

        @pl.when(jnp.logical_not(high))
        def _():
            pl.semaphore_signal(token.at[0], 1, device_id=(up, me), device_id_type=MESH)

    @pl.when((z >= NZ // 2) & (z < NZ - 1))
    def _():
        token_down()

    @pl.when(over)
    def _():
        pl.semaphore_wait(here, 1)

    mine = [cen[t].astype(F32) for t in range(TPG)] + [jnp.zeros((4, D), F32)]
    tiles[grp] = jnp.concatenate(mine, axis=0).astype(BF16)

    tile_copy(grp, up, zs.at[0, 0]).start()

    @pl.when(jnp.logical_not(low))
    def _():
        tile_copy(grp, down, zs.at[1, 0]).start()

    tile_copy(grp, twin, ks.at[0, 0]).start()

    @pl.loop(1, NX)
    def _(j):
        build(j)
        send_points(j)

    @pl.when(beside)
    def _():
        pl.semaphore_wait(here, 1)

        @pl.loop(1, NS)
        def _(k):
            @pl.when(peer(k) == 0)
            def _():
                point_copy(k).start()

    ids = lax.dot_general(
        own * (member_row + 1).astype(F32), at_rank, NT, precision=HI, preferred_element_type=F32
    )
    ids = (ids + 0.5).astype(I32)
    for o in range(NS):
        idsend[o] = ids[o : o + 1]

    @pl.loop(1, NS)
    def _(k):
        id_copy(k).start()

    got[me] = send[me]
    idgot[me] = idsend[me]

    @pl.when((z >= NZ // 4) & (z < NZ // 2))
    def _():
        token_down()

    reach = (NZ // 2, NZ // 2 - 1)

    def forward(way, step):
        dest, shift = ((up, NZ - step), (down, step))[way]
        entry = lax.rem(z + shift, NZ) * NC + core
        tile_copy(entry, dest, zs.at[way, 0]).wait_recv()

        @pl.when(step < reach[way])
        def _():
            tile_copy(entry, dest, zs.at[way, step]).start()

        tile_copy(entry, twin, ks.at[way, step]).start()

    @pl.loop(1, NZ // 2 + 2)
    def _(t):
        for late in range(2):
            for way in range(2):
                step = t - late
                if (late, way) == (0, 1):
                    step -= low.astype(I32)
                inside = (z, NZ - 1 - z)[way]
                due = step > inside if late else step <= inside

                @pl.when(due & (step >= 1) & (step <= reach[way]))
                def _():
                    forward(way, step)

        @pl.when((t == 1) & (z < NZ // 4))
        def _():
            token_down()

        @pl.when((t == 1) & low)
        def _():
            tile_copy(grp, down, zs.at[1, 0]).start()

    @pl.loop(0, NZ)
    def _(i):
        tile_copy(i * NC + 1 - core, twin, ks.at[0, 0]).wait_recv()

    line = iota((NS * 8, NS), 0)
    wanted = jnp.zeros((NS * 8, 1), I32)
    for k in range(K):
        match = line // 4 == iota((NS * 8, NS), 1) * K + k
        wanted += jnp.sum(jnp.where(match, cand[k : k + 1], 0), axis=1, keepdims=True)
    first = (wanted * 9363) >> 16
    code = first * 32 + (wanted - first * TPG) * 4 + lax.rem(iota((NS * 8, 1), 0), 4)
    pick = flag(code == iota((NS * 8, NG * 32), 1), BF16)

    @pl.loop(0, DH // 512)
    def _(i):
        halves = []
        for h in range(2):
            cols = pl.ds(pl.multiple_of(h * DH + i * 512, 512), 512)
            block = tiles[:, :, cols].reshape(NG * 32, 512)
            halves.append(jnp.dot(pick, block, preferred_element_type=F32).reshape(NS, 8, 512))
        both = jnp.concatenate(halves, axis=1).astype(BF16)
        csend[:, :, pl.ds(pl.multiple_of(i * 512, 512), 512)] = both

    def cen_copy(k):
        d = peer(k)
        return pltpu.make_async_remote_copy(
            src_ref=csend.at[d], dst_ref=cgot.at[me], send_sem=cs.at[k], recv_sem=cr.at[me],
            device_id=(grp, d), device_id_type=MESH,
        )

    @pl.loop(1, NS)
    def _(k):
        cen_copy(k).start()

    cgot[me] = csend[me]

    wide = pts[...].astype(F32)
    point_unit = unit(jnp.sum(wide * wide, axis=1, keepdims=True))

    def arrive(dst, sem, d):
        pltpu.make_async_remote_copy(
            src_ref=dst.at[d], dst_ref=dst.at[d], send_sem=ps.at[0], recv_sem=sem.at[d],
            device_id=(grp, d), device_id_type=MESH,
        ).wait_recv()

    @pl.loop(1, NS)
    def _(k):
        arrive(idgot, ids_r, peer(k))
        arrive(got, pr, peer(k))

    idm = jnp.concatenate([idgot[o] for o in range(NS)], axis=0).astype(F32)
    lane = iota((1, NS * 16), 1)
    mine = iota((NS, NS * 16), 0) == iota((NS, NS * 16), 1) // 16

    def scatter(q, a):
        quarter, slot = quarter_slot(a, lax.rem(lane, 16))
        slot = jnp.where(quarter == q, slot, -1)
        spread = flag(iota((TILE, NS * 16), 0) == slot)
        ids = jnp.dot(idm, spread, precision=HI, preferred_element_type=F32)
        row = jnp.sum(jnp.where(mine, ids, 0.0), axis=0, keepdims=True)
        row = (row + 0.5).astype(I32)
        return iota((CL * CAP, NS * 16), 0) + 1 == row

    full = flag(scatter(0, 0))
    grams = [jnp.zeros((CAP, CAP), F32) for _ in range(CL)]
    for q in range(Q):
        maps = [(a, flag(scatter(q, a), BF16)) for a in (q - 1, q) if 0 <= a < 3]

        def step(i, acc):
            cols = pl.ds(pl.multiple_of(i * 256, 256), 256)
            rows = None
            for a, m in maps:
                block = got[:, a * 16 : (a + 1) * 16, cols].reshape(NS * 16, 256)
                part = jnp.dot(m, block, preferred_element_type=F32)
                rows = part if rows is None else rows + part
            rows = rows.astype(BF16)
            out = []
            for c in range(CL):
                r = rows[c * CAP : (c + 1) * CAP]
                out.append(acc[c] + lax.dot_general(r, r, NT, preferred_element_type=F32))
            return out

        grams = lax.fori_loop(0, DQ // 256, step, grams)

    occupied = jnp.sum(full, axis=1, keepdims=True)
    diagonal = iota((CAP, CAP), 0) == iota((CAP, CAP), 1)
    bests = []
    for c in range(CL):
        g = grams[c]
        d = jnp.where(diagonal, g, 0.0)
        u_col = unit(jnp.sum(d, axis=1, keepdims=True))
        u_row = unit(jnp.sum(d, axis=0, keepdims=True))
        g = SCALE * g * u_col * u_row
        out_gram[c] = g
        others = flag((occupied[c * CAP : (c + 1) * CAP] > 0.5) & jnp.logical_not(diagonal))
        best = jnp.max(jnp.where(others > 0.5, g, -jnp.inf), axis=0, keepdims=True)
        some = jnp.max(others, axis=0, keepdims=True) > 0.5
        bests.append(jnp.where(some, best, 0.0))
    best = jnp.concatenate(bests, axis=1)

    rep = jnp.dot(
        jnp.broadcast_to(best, (8, CL * CAP)), full, precision=HI, preferred_element_type=F32
    )[0:1]
    slots = flag(lax.rem(iota((NS * 16, TILE), 0), 16) == iota((NS * 16, TILE), 1))
    rep = jnp.dot(jnp.where(mine, rep, 0.0), slots, precision=HI, preferred_element_type=F32)
    for o in range(NS):
        repsend[o] = rep[o : o + 1]

    def rep_copy(k):
        d = peer(k)
        return pltpu.make_async_remote_copy(
            src_ref=repsend.at[d], dst_ref=repgot.at[me], send_sem=rs.at[k], recv_sem=rr.at[me],
            device_id=(grp, d), device_id_type=MESH,
        )

    @pl.loop(1, NS)
    def _(k):
        rep_copy(k).start()

    repgot[me] = repsend[me]

    @pl.loop(1, NS)
    def _(k):
        point_copy(k).wait_send()
        id_copy(k).wait_send()

    tile_copy(grp, twin, ks.at[0, 0]).wait_send()
    for way in range(2):
        for step in range(reach[way]):
            tile_copy(grp, up, zs.at[way, step]).wait_send()
            tile_copy(grp, twin, ks.at[way, step + 1]).wait_send()

    out_scores[...] = jnp.zeros((PTS, K * TILE), F32)
    line = iota((NY * 8, 1), 0)
    base = lax.rem(line, NY * 4) // 4 * 16 + line // (NY * 4) * 4 + lax.rem(line, 4)
    column = line // (NY * 4) * TILE + lax.rem(line, NY * 4)

    def column_scores(j):
        xx = lax.rem(x - zigzag(j, NX) + NX, NX)

        @pl.loop(jnp.where(j == 0, 1, 0), NY)
        def _(i):
            arrive(cgot, cr, xx * NY + lax.rem(y - zigzag(i, NY) + NY, NY))

        def score(i, acc):
            dots, squares = acc
            for h in range(2):
                perm = flag(base + h * 8 == iota((NY * 8, NY * 16), 1), BF16)
                cols = pl.ds(pl.multiple_of(i * 512, 512), 512)
                block = cgot[pl.ds(xx * NY, NY), :, cols].reshape(NY * 16, 512)
                rows = jnp.dot(perm, block, preferred_element_type=F32)
                squares = squares + jnp.sum(rows * rows, axis=1, keepdims=True)
                p = pts[:, pl.ds(pl.multiple_of(h * DH + i * 512, 512), 512)]
                dots = dots + lax.dot_general(p, rows.astype(BF16), NT, preferred_element_type=F32)
            return dots, squares

        dots, squares = lax.fori_loop(
            0, DH // 512, score, (jnp.zeros((PTS, NY * 8), F32), jnp.zeros((NY * 8, 1), F32))
        )
        put = flag(column + xx * (NY * 4) == iota((NY * 8, K * TILE), 1))
        dots = SCALE * dots * point_unit * to_row(unit(squares))
        out_scores[...] += jnp.dot(dots, put, precision=HI, preferred_element_type=F32)

        @pl.loop(jnp.where(j == 0, 1, 0), NY)
        def _(i):
            cen_copy(j * NY + i).wait_send()

    @pl.loop(0, NX - 1)
    def _(j):
        column_scores(j)

    @pl.loop(1, NS)
    def _(k):
        arrive(repgot, rr, peer(k))

    rep = jnp.concatenate([repgot[o] for o in range(NS)], axis=0)
    back = jnp.dot(rep, at_rank, precision=HI, preferred_element_type=F32)
    out_best[...] = jnp.sum(own * back, axis=0, keepdims=True)

    @pl.loop(1, NS)
    def _(k):
        rep_copy(k).wait_send()

    column_scores(NX - 1)


def deliver(a, b, c, out_a, out_b, out_c):
    out_a[...] = a[...]
    out_b[...] = b[...]
    out_c[...] = c[...]


def on_device(points, centroids, candidates, assign, slot_index):
    cen = jnp.transpose(centroids, (1, 0, 2))
    dma = pltpu.SemaphoreType.DMA
    vmem = pl.BlockSpec(memory_space=pltpu.VMEM)
    outs = pl.pallas_call(
        kernel,
        out_shape=(
            jax.ShapeDtypeStruct((PTS, K * TILE), F32),
            jax.ShapeDtypeStruct((CL, CAP, CAP), F32),
            jax.ShapeDtypeStruct((1, PTS), F32),
        ),
        in_specs=[pl.BlockSpec(memory_space=pl.ANY)] + [vmem] * 4,
        out_specs=(vmem, vmem, vmem),
        scratch_shapes=[
            pltpu.VMEM((NS, 48, DQ), BF16),
            pltpu.VMEM((NS, 48, DQ), BF16),
            pltpu.VMEM((NG, 32, D), BF16),
            pltpu.VMEM((NS, 16, DH), BF16),
            pltpu.VMEM((NS, 16, DH), BF16),
            pltpu.VMEM((NS, 1, TILE), I32),
            pltpu.VMEM((NS, 1, TILE), I32),
            pltpu.VMEM((NS, 1, TILE), F32),
            pltpu.VMEM((NS, 1, TILE), F32),
            dma((NS,)), dma((NS,)), dma((NS,)), dma((NS,)),
            dma((2, NZ // 2)), dma((NG,)), dma((2, NZ // 2 + 1)),
            dma((NS,)), dma((NS,)), dma((NS,)), dma((NS,)),
            pltpu.SemaphoreType.REGULAR((2,)), pltpu.SemaphoreType.REGULAR,
            pltpu.VMEM((PTS, D), BF16), dma((1,)),
        ],
        compiler_params=pltpu.CompilerParams(
            collective_id=0, has_side_effects=True, vmem_limit_bytes=56 << 20
        ),
        name="fused",
    )(
        points, cen, candidates.T, assign.reshape(1, PTS),
        slot_index.reshape(1, PTS),
    )
    scores, gram, best = pl.pallas_call(
        deliver,
        out_shape=tuple(jax.ShapeDtypeStruct(o.shape, o.dtype) for o in outs),
        in_specs=[vmem] * 3,
        out_specs=(vmem,) * 3,
        compiler_params=pltpu.CompilerParams(vmem_limit_bytes=56 << 20),
        name="deliver",
    )(*outs)
    return scores, gram, best.reshape(PTS)


def solution(mesh):
    in_specs = (
        P(("grp", "shard"), None),
        P("shard", "grp", None),
        P("grp", None),
        P(("grp", "shard")),
        P(("grp", "shard")),
    )
    out_specs = (P(("grp", "shard"), None), P(("grp", "shard"), None, None), P(("grp", "shard")))
    return jax.shard_map(
        on_device, mesh=mesh, in_specs=in_specs, out_specs=out_specs, check_vma=False
    )
```

```python
import functools

import jax
import jax.numpy as jnp
from jax import lax
from jax.experimental import pallas as pl
from jax.experimental.pallas import tpu as pltpu
from jax.sharding import PartitionSpec as P

D = 4096
TILE = 128
K = 2
CAP = 128
PTS = 256
CL = 4
NX, NY, NZ, NC = 4, 8, 12, 2
NS = NX * NY
NG = NZ * NC
TPG = 7
EPS = 1e-06
SCALE = 64.0
Q = 4
DQ = D // Q
DH = D // 2
MESH = pl.DeviceIdType.MESH
HI = lax.Precision.HIGHEST
F32 = jnp.float32
BF16 = jnp.bfloat16
I32 = jnp.int32
NT = (((1,), (1,)), ((), ()))


def iota(shape, dim):
    return lax.broadcasted_iota(I32, shape, dim)


def flag(cond, dtype=F32):
    return jnp.where(cond, 1.0, 0.0).astype(dtype)


def unit(total):
    return lax.rsqrt(total * (1.0 / D) + EPS) * (1.0 / 64.0)


def to_row(column):
    n = column.shape[0]
    return jnp.sum(jnp.where(iota((n, n), 0) == iota((n, n), 1), column, 0), axis=0, keepdims=True)


def zigzag(i, n):
    return lax.rem(jnp.where(lax.rem(i, 2) == 1, (i + 1) // 2, n - i // 2), n)


def kernel(
    pts_hbm, cen, cand, asg, slt,
    out_scores, out_gram, out_best,
    send, got, tiles, csend, cgot, idsend, idgot, repsend, repgot,
    ps, pr, ids_s, ids_r, zs, zr, ks, cs, cr, rs, rr, token, here, pts, fs,
):
    fetch = pltpu.make_async_copy(pts_hbm, pts, fs.at[0])
    fetch.start()
    grp, me = lax.axis_index("grp"), lax.axis_index("shard")
    z, core = grp // NC, lax.rem(grp, NC)
    x, y = me // NY, lax.rem(me, NY)

    def peer(k):
        xx = lax.rem(x + zigzag(k // NY, NX), NX)
        yy = lax.rem(y + zigzag(lax.rem(k, NY), NY), NY)
        return xx * NY + yy

    up = lax.rem(z + 1, NZ) * NC + core
    down = lax.rem(z + NZ - 1, NZ) * NC + core
    twin = z * NC + (1 - core)
    low, high = z == 0, z == NZ - 1

    last = (grp == 0) & (me == 0)
    beside = (grp == 0) & (me != 0)
    over = (grp == 1) & (me == 0)
    above = (grp == NC) & (me == 0)
    barrier = pltpu.get_barrier_semaphore()

    @pl.when(jnp.logical_not(last))
    def _():
        @pl.loop(1, NS)
        def _(k):
            pl.semaphore_signal(barrier, 1, device_id=(grp, peer(k)), device_id_type=MESH)

        pl.semaphore_signal(barrier, 1, device_id=(twin, me), device_id_type=MESH)

        @pl.when(jnp.logical_not(high))
        def _():
            pl.semaphore_signal(barrier, 1, device_id=(up, me), device_id_type=MESH)

        @pl.when(jnp.logical_not(low))
        def _():
            pl.semaphore_signal(barrier, 1, device_id=(down, me), device_id_type=MESH)

    def tile_copy(entry, dest, ssem):
        return pltpu.make_async_remote_copy(
            src_ref=tiles.at[entry], dst_ref=tiles.at[entry], send_sem=ssem,
            recv_sem=zr.at[entry], device_id=(dest, me), device_id_type=MESH,
        )

    owner_row = lax.rem(asg[...] // CL, NS)
    member_row = lax.rem(asg[...], CL) * CAP + slt[...]
    own = flag(iota((NS, PTS), 0) == owner_row)
    before = flag(iota((PTS, PTS), 0) < iota((PTS, PTS), 1), BF16)
    ranks = jnp.dot(own.astype(BF16), before, preferred_element_type=F32)
    rank_row = jnp.sum(own * ranks, axis=0, keepdims=True).astype(I32)
    place_row = owner_row * 16 + rank_row
    at_rank = flag(iota((TILE, PTS), 0) == rank_row)

    def quarter_slot(a, i):
        p = a * 16 + i
        quarter = (p >= 12).astype(I32) + (p >= 24).astype(I32) + (p >= 36).astype(I32)
        return quarter, p - 12 * quarter

    def point_copy(k):
        d = peer(k)
        return pltpu.make_async_remote_copy(
            src_ref=send.at[d], dst_ref=got.at[me], send_sem=ps.at[k], recv_sem=pr.at[me],
            device_id=(grp, d), device_id_type=MESH,
        )

    def id_copy(k):
        d = peer(k)
        return pltpu.make_async_remote_copy(
            src_ref=idsend.at[d], dst_ref=idgot.at[me], send_sem=ids_s.at[k], recv_sem=ids_r.at[me],
            device_id=(grp, d), device_id_type=MESH,
        )

    def build(j):
        xx = lax.rem(x + zigzag(j, NX), NX)
        line = iota((NY * 16, 1), 0)
        for a in range(3):
            quarter, slot = quarter_slot(a, lax.rem(line, 16))
            code = xx * (NY * 16) + line // 16 * 16 + slot
            total = None
            for q in (a, a + 1):
                pick = flag(jnp.where(quarter == q, code, -1) == place_row, BF16)
                part = jnp.dot(pick, pts[:, q * DQ : (q + 1) * DQ], preferred_element_type=F32)
                total = part if total is None else total + part
            send[pl.ds(xx * NY, NY), a * 16 : (a + 1) * 16, :] = total.astype(BF16).reshape(NY, 16, DQ)

    fetch.wait()
    build(0)
    fewer = (low | high).astype(I32) + (beside | over | above).astype(I32)
    pl.semaphore_wait(barrier, NS - 1 + 3 - fewer)

    @pl.when(last)
    def _():
        @pl.loop(1, NS)
        def _(k):
            pl.semaphore_signal(here, 1, device_id=(grp, peer(k)), device_id_type=MESH)

        pl.semaphore_signal(here, 1, device_id=(twin, me), device_id_type=MESH)

    @pl.when(low)
    def _():
        pl.semaphore_signal(token.at[0], 1, device_id=(up, me), device_id_type=MESH)

    @pl.when(high)
    def _():
        pl.semaphore_signal(token.at[1], 1, device_id=(down, me), device_id_type=MESH)

    def send_points(j):
        @pl.loop(jnp.where(j == 0, 1, 0), NY)
        def _(i):
            @pl.when(jnp.logical_not(beside & (peer(j * NY + i) == 0)))
            def _():
                point_copy(j * NY + i).start()

    send_points(0)

    def token_down():
        pl.semaphore_wait(token.at[1], 1)

        @pl.when(jnp.logical_not(low))
        def _():
            pl.semaphore_signal(token.at[1], 1, device_id=(down, me), device_id_type=MESH)

    @pl.when(jnp.logical_not(low))
    def _():
        pl.semaphore_wait(token.at[0], 1)

        @pl.when(jnp.logical_not(high))
        def _():
            pl.semaphore_signal(token.at[0], 1, device_id=(up, me), device_id_type=MESH)

    @pl.when((z >= NZ // 2) & (z < NZ - 1))
    def _():
        token_down()

    @pl.when(over)
    def _():
        pl.semaphore_wait(here, 1)

    mine = [cen[t].astype(F32) for t in range(TPG)] + [jnp.zeros((4, D), F32)]
    tiles[grp] = jnp.concatenate(mine, axis=0).astype(BF16)

    tile_copy(grp, up, zs.at[0, 0]).start()

    @pl.when(jnp.logical_not(low))
    def _():
        tile_copy(grp, down, zs.at[1, 0]).start()

    tile_copy(grp, twin, ks.at[0, 0]).start()

    @pl.loop(1, NX)
    def _(j):
        build(j)
        send_points(j)

    @pl.when(beside)
    def _():
        pl.semaphore_wait(here, 1)

        @pl.loop(1, NS)
        def _(k):
            @pl.when(peer(k) == 0)
            def _():
                point_copy(k).start()

    ids = lax.dot_general(
        own * (member_row + 1).astype(F32), at_rank, NT, precision=HI, preferred_element_type=F32
    )
    ids = (ids + 0.5).astype(I32)
    for o in range(NS):
        idsend[o] = ids[o : o + 1]

    @pl.loop(1, NS)
    def _(k):
        id_copy(k).start()

    got[me] = send[me]
    idgot[me] = idsend[me]

    @pl.when((z >= NZ // 4) & (z < NZ // 2))
    def _():
        token_down()

    reach = (NZ // 2, NZ // 2 - 1)

    def forward(way, step):
        dest, shift = ((up, NZ - step), (down, step))[way]
        entry = lax.rem(z + shift, NZ) * NC + core
        tile_copy(entry, dest, zs.at[way, 0]).wait_recv()

        @pl.when(step < reach[way])
        def _():
            tile_copy(entry, dest, zs.at[way, step]).start()

        tile_copy(entry, twin, ks.at[way, step]).start()

    @pl.loop(1, NZ // 2 + 2)
    def _(t):
        for late in range(2):
            for way in range(2):
                step = t - late
                if (late, way) == (0, 1):
                    step -= low.astype(I32)
                inside = (z, NZ - 1 - z)[way]
                due = step > inside if late else step <= inside

                @pl.when(due & (step >= 1) & (step <= reach[way]))
                def _():
                    forward(way, step)

        @pl.when((t == 1) & (z < NZ // 4))
        def _():
            token_down()

        @pl.when((t == 1) & low)
        def _():
            tile_copy(grp, down, zs.at[1, 0]).start()

    @pl.loop(0, NZ)
    def _(i):
        tile_copy(i * NC + 1 - core, twin, ks.at[0, 0]).wait_recv()

    line = iota((NS * 8, NS), 0)
    wanted = jnp.zeros((NS * 8, 1), I32)
    for k in range(K):
        match = line // 4 == iota((NS * 8, NS), 1) * K + k
        wanted += jnp.sum(jnp.where(match, cand[k : k + 1], 0), axis=1, keepdims=True)
    first = (wanted * 9363) >> 16
    code = first * 32 + (wanted - first * TPG) * 4 + lax.rem(iota((NS * 8, 1), 0), 4)
    pick = flag(code == iota((NS * 8, NG * 32), 1), BF16)

    @pl.loop(0, DH // 512)
    def _(i):
        halves = []
        for h in range(2):
            cols = pl.ds(pl.multiple_of(h * DH + i * 512, 512), 512)
            block = tiles[:, :, cols].reshape(NG * 32, 512)
            halves.append(jnp.dot(pick, block, preferred_element_type=F32).reshape(NS, 8, 512))
        both = jnp.concatenate(halves, axis=1).astype(BF16)
        csend[:, :, pl.ds(pl.multiple_of(i * 512, 512), 512)] = both

    def cen_copy(k):
        d = peer(k)
        return pltpu.make_async_remote_copy(
            src_ref=csend.at[d], dst_ref=cgot.at[me], send_sem=cs.at[k], recv_sem=cr.at[me],
            device_id=(grp, d), device_id_type=MESH,
        )

    @pl.loop(1, NS)
    def _(k):
        cen_copy(NS - k).start()

    cgot[me] = csend[me]

    wide = pts[...].astype(F32)
    point_unit = unit(jnp.sum(wide * wide, axis=1, keepdims=True))

    def arrive(dst, sem, d):
        pltpu.make_async_remote_copy(
            src_ref=dst.at[d], dst_ref=dst.at[d], send_sem=ps.at[0], recv_sem=sem.at[d],
            device_id=(grp, d), device_id_type=MESH,
        ).wait_recv()

    @pl.loop(1, NS)
    def _(k):
        arrive(idgot, ids_r, peer(k))
        arrive(got, pr, peer(k))

    idm = jnp.concatenate([idgot[o] for o in range(NS)], axis=0).astype(F32)
    lane = iota((1, NS * 16), 1)
    mine = iota((NS, NS * 16), 0) == iota((NS, NS * 16), 1) // 16

    def scatter(q, a):
        quarter, slot = quarter_slot(a, lax.rem(lane, 16))
        slot = jnp.where(quarter == q, slot, -1)
        spread = flag(iota((TILE, NS * 16), 0) == slot)
        ids = jnp.dot(idm, spread, precision=HI, preferred_element_type=F32)
        row = jnp.sum(jnp.where(mine, ids, 0.0), axis=0, keepdims=True)
        row = (row + 0.5).astype(I32)
        return iota((CL * CAP, NS * 16), 0) + 1 == row

    full = flag(scatter(0, 0))
    grams = [jnp.zeros((CAP, CAP), F32) for _ in range(CL)]
    for q in range(Q):
        maps = [(a, flag(scatter(q, a), BF16)) for a in (q - 1, q) if 0 <= a < 3]

        def step(i, acc):
            cols = pl.ds(pl.multiple_of(i * 256, 256), 256)
            rows = None
            for a, m in maps:
                block = got[:, a * 16 : (a + 1) * 16, cols].reshape(NS * 16, 256)
                part = jnp.dot(m, block, preferred_element_type=F32)
                rows = part if rows is None else rows + part
            rows = rows.astype(BF16)
            out = []
            for c in range(CL):
                r = rows[c * CAP : (c + 1) * CAP]
                out.append(acc[c] + lax.dot_general(r, r, NT, preferred_element_type=F32))
            return out

        grams = lax.fori_loop(0, DQ // 256, step, grams)

    occupied = jnp.sum(full, axis=1, keepdims=True)
    diagonal = iota((CAP, CAP), 0) == iota((CAP, CAP), 1)
    bests = []
    for c in range(CL):
        g = grams[c]
        d = jnp.where(diagonal, g, 0.0)
        u_col = unit(jnp.sum(d, axis=1, keepdims=True))
        u_row = unit(jnp.sum(d, axis=0, keepdims=True))
        g = SCALE * g * u_col * u_row
        out_gram[c] = g
        others = flag((occupied[c * CAP : (c + 1) * CAP] > 0.5) & jnp.logical_not(diagonal))
        best = jnp.max(jnp.where(others > 0.5, g, -jnp.inf), axis=0, keepdims=True)
        some = jnp.max(others, axis=0, keepdims=True) > 0.5
        bests.append(jnp.where(some, best, 0.0))
    best = jnp.concatenate(bests, axis=1)

    rep = jnp.dot(
        jnp.broadcast_to(best, (8, CL * CAP)), full, precision=HI, preferred_element_type=F32
    )[0:1]
    slots = flag(lax.rem(iota((NS * 16, TILE), 0), 16) == iota((NS * 16, TILE), 1))
    rep = jnp.dot(jnp.where(mine, rep, 0.0), slots, precision=HI, preferred_element_type=F32)
    for o in range(NS):
        repsend[o] = rep[o : o + 1]

    def rep_copy(k):
        d = peer(k)
        return pltpu.make_async_remote_copy(
            src_ref=repsend.at[d], dst_ref=repgot.at[me], send_sem=rs.at[k], recv_sem=rr.at[me],
            device_id=(grp, d), device_id_type=MESH,
        )

    @pl.loop(1, NS)
    def _(k):
        rep_copy(k).start()

    repgot[me] = repsend[me]

    @pl.loop(1, NS)
    def _(k):
        point_copy(k).wait_send()
        id_copy(k).wait_send()

    tile_copy(grp, twin, ks.at[0, 0]).wait_send()
    for way in range(2):
        for step in range(reach[way]):
            tile_copy(grp, up, zs.at[way, step]).wait_send()
            tile_copy(grp, twin, ks.at[way, step + 1]).wait_send()

    out_scores[...] = jnp.zeros((PTS, K * TILE), F32)
    line = iota((NY * 8, 1), 0)
    base = lax.rem(line, NY * 4) // 4 * 16 + line // (NY * 4) * 4 + lax.rem(line, 4)
    column = line // (NY * 4) * TILE + lax.rem(line, NY * 4)

    def column_scores(j):
        xx = lax.rem(x - zigzag(j, NX) + NX, NX)

        @pl.loop(jnp.where(j == 0, 1, 0), NY)
        def _(i):
            arrive(cgot, cr, xx * NY + lax.rem(y - zigzag(i, NY) + NY, NY))

        def score(i, acc):
            dots, squares = acc
            for h in range(2):
                perm = flag(base + h * 8 == iota((NY * 8, NY * 16), 1), BF16)
                cols = pl.ds(pl.multiple_of(i * 512, 512), 512)
                block = cgot[pl.ds(xx * NY, NY), :, cols].reshape(NY * 16, 512)
                rows = jnp.dot(perm, block, preferred_element_type=F32)
                squares = squares + jnp.sum(rows * rows, axis=1, keepdims=True)
                p = pts[:, pl.ds(pl.multiple_of(h * DH + i * 512, 512), 512)]
                dots = dots + lax.dot_general(p, rows.astype(BF16), NT, preferred_element_type=F32)
            return dots, squares

        dots, squares = lax.fori_loop(
            0, DH // 512, score, (jnp.zeros((PTS, NY * 8), F32), jnp.zeros((NY * 8, 1), F32))
        )
        put = flag(column + xx * (NY * 4) == iota((NY * 8, K * TILE), 1))
        dots = SCALE * dots * point_unit * to_row(unit(squares))
        out_scores[...] += jnp.dot(dots, put, precision=HI, preferred_element_type=F32)

        @pl.loop(jnp.where(j == 0, 1, 0), NY)
        def _(i):
            cen_copy(j * NY + i).wait_send()

    @pl.loop(0, NX - 1)
    def _(j):
        column_scores(NX - 1 - j)

    @pl.loop(1, NS)
    def _(k):
        arrive(repgot, rr, peer(k))

    rep = jnp.concatenate([repgot[o] for o in range(NS)], axis=0)
    back = jnp.dot(rep, at_rank, precision=HI, preferred_element_type=F32)
    out_best[...] = jnp.sum(own * back, axis=0, keepdims=True)

    @pl.loop(1, NS)
    def _(k):
        rep_copy(k).wait_send()

    column_scores(0)


def deliver(a, b, c, out_a, out_b, out_c):
    out_a[...] = a[...]
    out_b[...] = b[...]
    out_c[...] = c[...]


def on_device(points, centroids, candidates, assign, slot_index):
    cen = jnp.transpose(centroids, (1, 0, 2))
    dma = pltpu.SemaphoreType.DMA
    vmem = pl.BlockSpec(memory_space=pltpu.VMEM)
    outs = pl.pallas_call(
        kernel,
        out_shape=(
            jax.ShapeDtypeStruct((PTS, K * TILE), F32),
            jax.ShapeDtypeStruct((CL, CAP, CAP), F32),
            jax.ShapeDtypeStruct((1, PTS), F32),
        ),
        in_specs=[pl.BlockSpec(memory_space=pl.ANY)] + [vmem] * 4,
        out_specs=(vmem, vmem, vmem),
        scratch_shapes=[
            pltpu.VMEM((NS, 48, DQ), BF16),
            pltpu.VMEM((NS, 48, DQ), BF16),
            pltpu.VMEM((NG, 32, D), BF16),
            pltpu.VMEM((NS, 16, DH), BF16),
            pltpu.VMEM((NS, 16, DH), BF16),
            pltpu.VMEM((NS, 1, TILE), I32),
            pltpu.VMEM((NS, 1, TILE), I32),
            pltpu.VMEM((NS, 1, TILE), F32),
            pltpu.VMEM((NS, 1, TILE), F32),
            dma((NS,)), dma((NS,)), dma((NS,)), dma((NS,)),
            dma((2, NZ // 2)), dma((NG,)), dma((2, NZ // 2 + 1)),
            dma((NS,)), dma((NS,)), dma((NS,)), dma((NS,)),
            pltpu.SemaphoreType.REGULAR((2,)), pltpu.SemaphoreType.REGULAR,
            pltpu.VMEM((PTS, D), BF16), dma((1,)),
        ],
        compiler_params=pltpu.CompilerParams(
            collective_id=0, has_side_effects=True, vmem_limit_bytes=56 << 20
        ),
        name="fused",
    )(
        points, cen, candidates.T, assign.reshape(1, PTS),
        slot_index.reshape(1, PTS),
    )
    scores, gram, best = pl.pallas_call(
        deliver,
        out_shape=tuple(jax.ShapeDtypeStruct(o.shape, o.dtype) for o in outs),
        in_specs=[vmem] * 3,
        out_specs=(vmem,) * 3,
        compiler_params=pltpu.CompilerParams(vmem_limit_bytes=56 << 20),
        name="deliver",
    )(*outs)
    return scores, gram, best.reshape(PTS)


def solution(mesh):
    in_specs = (
        P(("grp", "shard"), None),
        P("shard", "grp", None),
        P("grp", None),
        P(("grp", "shard")),
        P(("grp", "shard")),
    )
    out_specs = (P(("grp", "shard"), None), P(("grp", "shard"), None, None), P(("grp", "shard")))
    return jax.shard_map(
        on_device, mesh=mesh, in_specs=in_specs, out_specs=out_specs, check_vma=False
    )
```
